512 devices in a mesh: seq: 64 (over z, y), mp: 8 (over x, core).
Axes of the slice: x: 4, y: 4, z: 16, core: 2. Of those that a mesh axis runs over, the one named last changes fastest.
Arguments:
- shared_qk: bfloat16 [8192, 4096], P('seq', 'mp'), may hold values from -40 to 40
- values: bfloat16 [8192, 4096], P('seq', 'mp'), may hold values from -6 to 6
- buckets: int32 [8192, 32], P('seq', 'mp'), may hold values from 0 to 63, as said below
- counts: int32 [64, 32, 64], P(None, 'mp'), may hold values from 0 to 4, as said below
- w_out: bfloat16 [4096, 4096], P('mp'), may hold values from -0.09375 to 0.09375
Outputs:
- projected: bfloat16 [8192, 4096], P('seq', 'mp')
The draws below stay inside these ranges and needn't reach their ends.
Inputs may be any that keep to these rules, and one draw needn't show every extreme that they name: `buckets`: in each head at most 4 tokens among rows d * 128 to (d + 1) * 128 - 1 name one bucket, and in each head one bucket is named by exactly 4 tokens of every such group of rows. counts[d, h, b] is the number of rows among d * 128 to (d + 1) * 128 - 1 whose bucket in head h is b.
All inputs are finite; a program needn't handle non-finite values.
Results may differ from the reference program's by a relative error of at most 0.0057.
Values may be sent and summed in bfloat16 or wider, within the bound.
A program may use at most 64 MiB of HBM per device.

```python
import math
import jax
import jax.numpy as jnp
from jax import lax

D = 4096
H = 32
DH = 128
BLOCK = 256
TOK_DEV = 128
TOKENS = 8192
NBK = 64
CAP = 4
SLOTS = 256


def routing_tables(key):
    seeded = jax.random.fold_in(key, 1234)
    key_bias, key_full, key_jitter, key_perm = jax.random.split(seeded, 4)
    tickets = NBK * CAP
    bucket_range = jnp.arange(NBK)
    bucket_bias = jax.random.randint(key_bias, (H, NBK), 0, 2048)
    full_bucket = jax.random.randint(key_full, (H,), 0, NBK)
    bucket_bias = jnp.where(bucket_range[None, :] == full_bucket[:, None], 16384, bucket_bias)
    ticket_bucket = jnp.arange(tickets) // CAP
    jitter = jax.random.randint(key_jitter, (NBK, H, tickets), 0, 1024)
    ticket_score = (bucket_bias[:, ticket_bucket][None] + jitter) * 4096 + jnp.arange(tickets)[None, None, :]
    unused_scores, chosen = lax.top_k(ticket_score, TOK_DEV)
    chosen_bucket = (chosen // CAP).astype(jnp.int32).reshape(NBK * H, TOK_DEV)
    counts = jax.vmap(lambda row: jnp.bincount(row, length=NBK))(chosen_bucket).reshape(NBK, H, NBK)
    perm_keys = jax.random.split(key_perm, NBK * H)
    perms = jax.vmap(lambda single: jax.random.permutation(single, TOK_DEV))(perm_keys)
    shuffled = jnp.take_along_axis(chosen_bucket, perms, axis=1).reshape(NBK, H, TOK_DEV)
    buckets = jnp.transpose(shuffled, (0, 2, 1)).reshape(TOKENS, H)
    return (buckets.astype(jnp.int32), counts.astype(jnp.int32))


def draw_buckets(key, part):
    return routing_tables(key)[0]


def draw_counts(key, part):
    return routing_tables(key)[1]


def draw_shared_qk(key, part):
    key_base = jax.random.fold_in(jax.random.fold_in(key, 77), 0)
    normal_part = jax.random.normal(key_base, (TOKENS, H, DH), jnp.float32)
    return jnp.clip(normal_part, -40.0, 40.0).reshape(TOKENS, H * DH).astype(jnp.bfloat16)


def block_levels(rng, extent, cuts, smallest, top_value):
    factor_of, own = 1.0, jax.random.fold_in(rng, 6)
    for axis_at, shards_of in cuts:
        heights = jnp.exp(jax.random.uniform(jax.random.fold_in(own, axis_at), (shards_of,), jnp.float32, smallest / len(cuts), top_value / len(cuts)))
        factor_of = factor_of * jnp.repeat(heights, extent[axis_at] // shards_of).reshape([-1 if axis == axis_at else 1 for axis in range(len(extent))])
    return factor_of


def gaussian(own_key, shape, width, bound, cuts=(), held_as=jnp.bfloat16):
    drawn = jax.random.normal(own_key, shape, jnp.float32) * width
    if len(cuts) > 0:
        drawn = block_levels(own_key, shape, cuts, -0.22, 0.18) * drawn
    return jnp.clip(drawn, min=-bound, max=bound).astype(held_as)


def setup_inputs(seed: int = 0) -> dict:
    arg_keys = jax.random.split(jax.random.key(seed), 6)
    shared_qk = draw_shared_qk(jax.random.fold_in(arg_keys[5], 71), 0)
    values = gaussian(arg_keys[1], (TOKENS, H * DH), 1.0, 6.0, ((0, 64), (1, 8)))
    buckets = draw_buckets(jax.random.fold_in(arg_keys[5], 71), 0)
    counts = draw_counts(jax.random.fold_in(arg_keys[5], 71), 0)
    w_out = gaussian(arg_keys[4], (H * DH, D), (H * DH) ** -0.5, 0.09375, ((0, 8),))
    return {"shared_qk": shared_qk, "values": values, "buckets": buckets, "counts": counts, "w_out": w_out}


SELF_SCORE = -100000.0

def block_attention(queries, window, window_live):
    head_dim = queries.shape[-1]
    block_rows = queries.shape[-2]
    key_rows = window[..., :head_dim].astype(jnp.float32)
    value_rows = window[..., head_dim:].astype(jnp.float32)
    scores = jnp.einsum('cqd,ckd->cqk', queries.astype(jnp.float32), key_rows) * (1.0 / math.sqrt(head_dim))
    query_place = jnp.arange(block_rows)[:, None] + block_rows
    key_place = jnp.arange(2 * block_rows)[None, :]
    itself = query_place == key_place
    scores = jnp.where(itself[None], SELF_SCORE, scores)
    allowed = window_live[:, None, :] | itself[None]
    row_max = lax.optimization_barrier(jnp.max(jnp.where(allowed, scores, -1e+30), axis=-1, keepdims=True))
    exp_terms = jnp.where(allowed, jnp.exp(scores - row_max), 0.0)
    weights = (exp_terms / lax.optimization_barrier(jnp.sum(exp_terms, axis=-1, keepdims=True))).astype(jnp.bfloat16)
    attended = jnp.einsum('cqk,ckd->cqd', weights.astype(jnp.float32), value_rows)
    return attended.astype(jnp.bfloat16)

def attend_head(qk_head, value_head, bucket_head, size_head):
    positions = jnp.arange(TOKENS).astype(jnp.int32)
    token_order = jnp.argsort(bucket_head * TOKENS + positions).astype(jnp.int32)
    sorted_bucket = bucket_head[token_order]
    seg_starts = (jnp.cumsum(size_head) - size_head).astype(jnp.int32)
    sorted_rank = (positions - seg_starts[sorted_bucket]).astype(jnp.int32)
    slot_index = (sorted_bucket * SLOTS + sorted_rank).astype(jnp.int32)
    packed = jnp.concatenate([qk_head, value_head], axis=1)
    layout = jnp.zeros((NBK * SLOTS, 2 * DH), packed.dtype).at[slot_index].set(packed[token_order])
    layout = layout.reshape(NBK, SLOTS, 2 * DH)
    live = jnp.arange(SLOTS)[None, :] < size_head[:, None]
    rank_index = (size_head[:, None] - BLOCK + jnp.arange(BLOCK)[None, :]).astype(jnp.int32)
    tail_live = rank_index >= 0
    seg_range = jnp.arange(NBK)[:, None]
    tail_rows = layout[seg_range, jnp.maximum(rank_index, 0)]
    tail_rows = jnp.where(tail_live[..., None], tail_rows, jnp.zeros((), tail_rows.dtype))
    prev_rows = jnp.roll(tail_rows, 1, axis=0)
    prev_live = jnp.roll(tail_live, 1, axis=0)
    keys_all = jnp.concatenate([prev_rows, layout], axis=1)
    live_all = jnp.concatenate([prev_live, live], axis=1)
    block_count = SLOTS // BLOCK
    window = jnp.concatenate([keys_all[:, :SLOTS].reshape(NBK, block_count, BLOCK, 2 * DH), keys_all[:, BLOCK:].reshape(NBK, block_count, BLOCK, 2 * DH)], axis=2)
    window_live = jnp.concatenate([live_all[:, :SLOTS].reshape(NBK, block_count, BLOCK), live_all[:, BLOCK:].reshape(NBK, block_count, BLOCK)], axis=2)
    queries = layout[..., :DH].reshape(NBK * block_count, BLOCK, DH)
    attended = block_attention(queries, window.reshape(NBK * block_count, 2 * BLOCK, 2 * DH), window_live.reshape(NBK * block_count, 2 * BLOCK))
    out_layout = attended.reshape(NBK * SLOTS, DH)
    token_slot = jnp.zeros((TOKENS,), jnp.int32).at[token_order].set(slot_index)
    return out_layout[token_slot]

def reference(shared_qk, values, buckets, counts, w_out):
    qk_heads = jnp.transpose(shared_qk.reshape(TOKENS, H, DH), (1, 0, 2))
    value_heads = jnp.transpose(values.reshape(TOKENS, H, DH), (1, 0, 2))
    bucket_heads = buckets.T.astype(jnp.int32)
    sizes = lax.optimization_barrier(jnp.sum(counts, axis=0)).astype(jnp.int32)
    per_head = lax.map(lambda item: attend_head(item[0], item[1], item[2], item[3]), (qk_heads, value_heads, bucket_heads, sizes))
    attended = jnp.transpose(per_head, (1, 0, 2)).reshape(TOKENS, H * DH)
    projected = jnp.dot(attended.astype(jnp.float32), w_out.astype(jnp.float32), preferred_element_type=jnp.float32)
    return projected.astype(jnp.bfloat16)
```

```python
import functools
import math

import jax
import jax.numpy as jnp
from jax import lax
from jax.experimental import pallas as pl
from jax.experimental.pallas import tpu as pltpu
from jax.sharding import PartitionSpec as P

CAP = 4
SELF_SCORE = -100000.0
DEAD = -1e30
BF16 = jnp.bfloat16
F32 = jnp.float32
MESH = pl.DeviceIdType.MESH


def iota(shape, dim):
    return lax.broadcasted_iota(jnp.int32, shape, dim)


def one_hot(mask):
    return jnp.where(mask, 1.0, 0.0).astype(BF16)


def dot(a, b):
    return jnp.dot(a, b, preferred_element_type=F32)


def layer_kernel(
    planes, heads, chips, tok, dim,
    qk_ref, val_ref, buckets_ref, counts_ref, w_ref, out_ref,
    w_buf, out_pack, in_pack, rows_buf, prev_buf, att_buf, out_ret, in_ret, tok_buf, pick_buf,
    pair_out, pair_in, chip_out, chip_in,
    w_sem, pack_send, pack_recv, next_send, next_recv, ret_send, ret_recv,
    pair_send, pair_recv, chip_send, chip_recv,
):
    devices = planes * heads
    slots = devices * CAP
    unit = heads * CAP
    groups = devices // 16
    span = 16 * unit
    part = 16 * CAP
    block = w_ref.shape[1] // (2 * chips)
    me = lax.axis_index("seq")
    mp = lax.axis_index("mp")
    z, y = me // heads, lax.rem(me, heads)
    x, core = mp // 2, lax.rem(mp, 2)

    load_w = pltpu.make_async_copy(w_ref, w_buf, w_sem)
    load_w.start()

    barrier = pltpu.get_barrier_semaphore()

    def greet(k, carry):
        other = lax.rem(me + k, devices)
        pl.semaphore_signal(barrier, inc=1, device_id=(other, mp), device_id_type=MESH)
        return carry

    lax.fori_loop(1, devices, greet, 0)
    pl.semaphore_signal(barrier, inc=1, device_id=(me, x * 2 + 1 - core), device_id_type=MESH)
    for off in range(1, chips):
        there = lax.rem(x + off, chips) * 2 + core
        pl.semaphore_signal(barrier, inc=1, device_id=(me, there), device_id_type=MESH)

    eye = iota((tok, tok), 0) == iota((tok, tok), 1)
    before = iota((tok, tok), 0) < iota((tok, tok), 1)
    after = iota((tok, tok), 0) > iota((tok, tok), 1)
    for h in range(heads):
        b_col = buckets_ref[:, h : h + 1]
        b_row = jnp.sum(jnp.where(eye, b_col, 0), axis=0, keepdims=True)
        same = b_col == b_row
        rank_row = jnp.sum(jnp.where(same & before, 1, 0), axis=0, keepdims=True)
        rank_col = jnp.sum(jnp.where(same & after, 1, 0), axis=1, keepdims=True)
        place = one_hot(iota((slots, tok), 0) == b_row * CAP + rank_row)
        pick_buf[h] = one_hot(iota((tok, slots), 1) == b_col * CAP + rank_col)
        cols = slice(h * dim, (h + 1) * dim)
        rows = slice(h * slots, (h + 1) * slots)
        out_pack[rows, :dim] = dot(place, qk_ref[:, cols]).astype(BF16)
        out_pack[rows, dim:] = dot(place, val_ref[:, cols]).astype(BF16)

    pl.semaphore_wait(barrier, devices - 1 + chips)

    def peer(i):
        a = i // heads
        half = planes // 2
        dz = jnp.where(lax.rem(a, 2) == 1, half - (a + 1) // 2, half + a // 2)
        pz = lax.rem(z + dz, planes)
        py = lax.rem(y + heads - 1 - lax.rem(i, heads), heads)
        return pz, py

    def pack_copy(i):
        pz, py = peer(i)
        src = pl.multiple_of(py * slots + pz * unit, unit)
        dst = pl.multiple_of(me * unit, unit)
        return pltpu.make_async_remote_copy(
            src_ref=out_pack.at[pl.ds(src, unit)],
            dst_ref=in_pack.at[pl.ds(dst, unit)],
            send_sem=pack_send,
            recv_sem=pack_recv.at[me // 16],
            device_id=(pz * heads + py, mp),
            device_id_type=MESH,
        )

    def send_pack(i, carry):
        pack_copy(i).start()
        return carry

    lax.fori_loop(0, devices - 1, send_pack, 0)
    own_src = pl.multiple_of(y * slots + z * unit, unit)
    own_dst = pl.multiple_of(me * unit, unit)
    pltpu.make_async_copy(
        out_pack.at[pl.ds(own_src, unit)], in_pack.at[pl.ds(own_dst, unit)], pack_recv.at[me // 16]
    ).start()

    counts = counts_ref[:, y, :]
    spread = (iota((devices, slots), 1) // CAP) == iota((devices, slots), 0)
    rank = lax.rem(iota((1, slots), 1), CAP)
    dead = []
    for j in range(-1, heads):
        b = lax.rem(z * heads + j + devices, devices)
        column = jnp.sum(jnp.where(iota(counts.shape, 1) == b, counts, 0), axis=1, keepdims=True)
        row = jnp.sum(jnp.where(spread, column, 0), axis=0, keepdims=True)
        dead.append(jnp.where(rank < row, 0.0, DEAD))

    def by_bucket(i):
        return (i // CAP) % 16 * unit + i // part * CAP + i % CAP

    order = one_hot(by_bucket(iota((span, span), 0)) == iota((span, span), 1))
    order_back = one_hot(by_bucket(iota((span, span), 1)) == iota((span, span), 0))

    next_z = lax.rem(z + 1, planes)
    for g in range(groups):
        here = in_pack.at[g * span : (g + 1) * span]
        pltpu.make_async_copy(here, here, pack_recv.at[g]).wait()
        arranged = dot(order, here[...]).astype(BF16)
        rows = slice(g * part, (g + 1) * part)
        for j in range(heads):
            rows_buf[j, rows, :] = arranged[j * part : (j + 1) * part]
        pltpu.make_async_remote_copy(
            src_ref=rows_buf.at[heads - 1, rows],
            dst_ref=prev_buf.at[rows],
            send_sem=next_send,
            recv_sem=next_recv,
            device_id=(next_z * heads + y, mp),
            device_id_type=MESH,
        ).start()

    itself = iota((slots, slots), 0) == iota((slots, slots), 1)
    scale = 1.0 / math.sqrt(dim)

    def attend(j, prev):
        q = rows_buf[j, :, :dim]
        v = rows_buf[j, :, dim:]
        trans = (((1,), (1,)), ((), ()))
        own = lax.dot_general(q, q, trans, preferred_element_type=F32)
        own = jnp.where(itself, SELF_SCORE, own * scale + dead[j + 1])
        far = lax.dot_general(q, prev[:, :dim], trans, preferred_element_type=F32) * scale + dead[j]
        top = jnp.maximum(jnp.max(own, axis=1, keepdims=True), jnp.max(far, axis=1, keepdims=True))
        own = jnp.exp(own - top)
        far = jnp.exp(far - top)
        total = jnp.sum(own, axis=1, keepdims=True) + jnp.sum(far, axis=1, keepdims=True)
        share = 1.0 / total
        att = dot((own * share).astype(BF16), v) + dot((far * share).astype(BF16), prev[:, dim:])
        att_buf[j] = att.astype(BF16)

    for j in range(1, heads):
        attend(j, rows_buf[j - 1])
    pltpu.make_async_copy(prev_buf, prev_buf, next_recv).wait()
    attend(0, prev_buf[...])

    for g in range(groups):
        rows = slice(g * part, (g + 1) * part)
        mine = jnp.concatenate([att_buf[j, rows, :] for j in range(heads)], axis=0)
        out_ret[g * span : (g + 1) * span, :] = dot(order_back, mine).astype(BF16)

    def ret_copy(i):
        pz, py = peer(i)
        there = pz * heads + py
        return pltpu.make_async_remote_copy(
            src_ref=out_ret.at[pl.ds(pl.multiple_of(there * unit, unit), unit)],
            dst_ref=in_ret.at[pl.ds(own_src, unit)],
            send_sem=ret_send,
            recv_sem=ret_recv.at[y],
            device_id=(there, mp),
            device_id_type=MESH,
        )

    def send_ret(i, carry):
        ret_copy(i).start()
        return carry

    lax.fori_loop(0, devices - 1, send_ret, 0)
    pltpu.make_async_copy(
        out_ret.at[pl.ds(own_dst, unit)], in_ret.at[pl.ds(own_src, unit)], ret_recv.at[y]
    ).start()

    load_w.wait()
    for h in range(heads):
        here = in_ret.at[h * slots : (h + 1) * slots]
        pltpu.make_async_copy(here, here, ret_recv.at[h]).wait()
        tok_buf[:, h * dim : (h + 1) * dim] = dot(pick_buf[h], here[...]).astype(BF16)

    def share_of(m):
        return dot(tok_buf[...], w_buf[:, pl.ds(pl.multiple_of(m * block, block), block)])

    offsets = sorted(range(chips), key=lambda off: -min(off, chips - off))
    for k, off in enumerate(offsets):
        cx = lax.rem(x + off, chips)
        pair_out[k] = share_of(cx * 2 + 1 - core).astype(BF16)
        pltpu.make_async_remote_copy(
            src_ref=pair_out.at[k],
            dst_ref=pair_in.at[k],
            send_sem=pair_send,
            recv_sem=pair_recv.at[k],
            device_id=(me, x * 2 + 1 - core),
            device_id_type=MESH,
        ).start()
    total = None
    for k, off in enumerate(offsets):
        cx = lax.rem(x + off, chips)
        total = share_of(cx * 2 + core)
        pltpu.make_async_copy(pair_in.at[k], pair_in.at[k], pair_recv.at[k]).wait()
        total = total + pair_in[k].astype(F32)
        if off:
            chip_out[k] = total.astype(BF16)
            pltpu.make_async_remote_copy(
                src_ref=chip_out.at[k],
                dst_ref=chip_in.at[k],
                send_sem=chip_send,
                recv_sem=chip_recv.at[k],
                device_id=(me, cx * 2 + core),
                device_id_type=MESH,
            ).start()
    for k in range(chips - 1):
        pltpu.make_async_copy(chip_in.at[k], chip_in.at[k], chip_recv.at[k]).wait()
        total = total + chip_in[k].astype(F32)
    out_ref[...] = total.astype(BF16)

    most = (devices - 1) * unit
    pltpu.make_async_copy(out_pack.at[:most], out_pack.at[:most], pack_send).wait()
    pltpu.make_async_copy(prev_buf, prev_buf, next_send).wait()
    pltpu.make_async_copy(out_ret.at[:most], out_ret.at[:most], ret_send).wait()
    pltpu.make_async_copy(pair_out, pair_out, pair_send).wait()
    pltpu.make_async_copy(chip_out, chip_out, chip_send).wait()


def local(planes, chips, shared_qk, values, buckets, counts, w_out):
    tok, width = shared_qk.shape
    heads = buckets.shape[1]
    dim = width // heads
    devices = planes * heads
    slots = devices * CAP
    groups = devices // 16
    block = w_out.shape[1] // (2 * chips)
    vmem = pl.BlockSpec(memory_space=pltpu.VMEM)
    dma = pltpu.SemaphoreType.DMA
    return pl.pallas_call(
        functools.partial(layer_kernel, planes, heads, chips, tok, dim),
        out_shape=jax.ShapeDtypeStruct((tok, block), BF16),
        in_specs=[vmem, vmem, vmem, vmem, pl.BlockSpec(memory_space=pl.ANY)],
        out_specs=vmem,
        scratch_shapes=[
            pltpu.VMEM(w_out.shape, BF16),
            pltpu.VMEM((heads * slots, 2 * dim), BF16),
            pltpu.VMEM((heads * slots, 2 * dim), BF16),
            pltpu.VMEM((heads, slots, 2 * dim), BF16),
            pltpu.VMEM((slots, 2 * dim), BF16),
            pltpu.VMEM((heads, slots, dim), BF16),
            pltpu.VMEM((heads * slots, dim), BF16),
            pltpu.VMEM((heads * slots, dim), BF16),
            pltpu.VMEM((tok, heads * dim), BF16),
            pltpu.VMEM((heads, tok, slots), BF16),
            pltpu.VMEM((chips, tok, block), BF16),
            pltpu.VMEM((chips, tok, block), BF16),
            pltpu.VMEM((chips - 1, tok, block), BF16),
            pltpu.VMEM((chips - 1, tok, block), BF16),
            dma,
            dma,
            dma((groups,)),
            dma,
            dma,
            dma,
            dma((heads,)),
            dma,
            dma((chips,)),
            dma,
            dma((chips - 1,)),
        ],
        compiler_params=pltpu.CompilerParams(
            collective_id=0, has_side_effects=True, vmem_limit_bytes=32 * 1024 * 1024
        ),
    )(shared_qk, values, buckets, counts, w_out)


def solution(mesh):
    placed = (P("seq", "mp"), P("seq", "mp"), P("seq", "mp"), P(None, "mp", None), P("mp", None))
    heads = 4
    planes = mesh.shape["seq"] // heads
    chips = mesh.shape["mp"] // 2
    return jax.shard_map(
        functools.partial(local, planes, chips),
        mesh=mesh, in_specs=placed, out_specs=P("seq", "mp"), check_vma=False,
    )
```

```python
import functools
import math

import jax
import jax.numpy as jnp
from jax import lax
from jax.experimental import pallas as pl
from jax.experimental.pallas import tpu as pltpu
from jax.sharding import PartitionSpec as P

CAP = 4
SELF_SCORE = -100000.0
DEAD = -1e30
BF16 = jnp.bfloat16
F32 = jnp.float32
MESH = pl.DeviceIdType.MESH


def iota(shape, dim):
    return lax.broadcasted_iota(jnp.int32, shape, dim)


def one_hot(mask):
    return jnp.where(mask, 1.0, 0.0).astype(BF16)


def dot(a, b):
    return jnp.dot(a, b, preferred_element_type=F32)


def layer_kernel(
    planes, heads, chips, tok, dim,
    qk_hbm, val_hbm, buckets_hbm, counts_hbm, w_hbm, out_ref,
    qk_ref, val_ref, buckets_ref, counts_ref, w_buf, out_pack, in_pack, rows_buf, prev_buf, att_buf, out_ret, in_ret, tok_buf, pick_buf,
    pair_out, pair_in, chip_out, chip_in,
    load_sem, w_sem, pack_send, pack_recv, next_send, next_recv, ret_send, ret_recv,
    pair_send, pair_recv, chip_send, chip_recv,
):
    devices = planes * heads
    slots = devices * CAP
    unit = heads * CAP
    groups = devices // 16
    span = 16 * unit
    part = 16 * CAP
    block = w_hbm.shape[1] // (2 * chips)
    me = lax.axis_index("seq")
    mp = lax.axis_index("mp")
    z, y = me // heads, lax.rem(me, heads)
    x, core = mp // 2, lax.rem(mp, 2)

    loads = [
        pltpu.make_async_copy(buckets_hbm, buckets_ref, load_sem.at[0]),
        pltpu.make_async_copy(qk_hbm, qk_ref, load_sem.at[1]),
        pltpu.make_async_copy(val_hbm, val_ref, load_sem.at[2]),
        pltpu.make_async_copy(counts_hbm, counts_ref, load_sem.at[3]),
        pltpu.make_async_copy(w_hbm, w_buf, w_sem),
    ]
    for load in loads:
        load.start()

    barrier = pltpu.get_barrier_semaphore()

    def greet(k, carry):
        other = lax.rem(me + k, devices)
        pl.semaphore_signal(barrier, inc=1, device_id=(other, mp), device_id_type=MESH)
        return carry

    lax.fori_loop(1, devices, greet, 0)
    pl.semaphore_signal(barrier, inc=1, device_id=(me, x * 2 + 1 - core), device_id_type=MESH)
    for off in range(1, chips):
        there = lax.rem(x + off, chips) * 2 + core
        pl.semaphore_signal(barrier, inc=1, device_id=(me, there), device_id_type=MESH)

    eye = iota((tok, tok), 0) == iota((tok, tok), 1)
    before = iota((tok, tok), 0) < iota((tok, tok), 1)
    for load in loads[:3]:
        load.wait()
    for h in range(heads):
        b_row = buckets_ref[h : h + 1, :]
        b_col = jnp.sum(jnp.where(eye, b_row, 0), axis=1, keepdims=True)
        same = b_col == b_row
        rank_row = jnp.sum(jnp.where(same & before, 1, 0), axis=0, keepdims=True)
        place = one_hot(iota((slots, tok), 0) == b_row * CAP + rank_row)
        cols = slice(h * dim, (h + 1) * dim)
        rows = slice(h * slots, (h + 1) * slots)
        out_pack[rows, :dim] = dot(place, qk_ref[:, cols]).astype(BF16)
        out_pack[rows, dim:] = dot(place, val_ref[:, cols]).astype(BF16)

    pl.semaphore_wait(barrier, devices - 1 + chips)

    def peer(i):
        a = i // heads
        half = planes // 2
        dz = jnp.where(lax.rem(a, 2) == 1, half - (a + 1) // 2, half + a // 2)
        pz = lax.rem(z + dz, planes)
        py = lax.rem(y + heads - 1 - lax.rem(i, heads), heads)
        return pz, py

    def pack_copy(i):
        pz, py = peer(i)
        src = pl.multiple_of(py * slots + pz * unit, unit)
        dst = pl.multiple_of(me * unit, unit)
        return pltpu.make_async_remote_copy(
            src_ref=out_pack.at[pl.ds(src, unit)],
            dst_ref=in_pack.at[pl.ds(dst, unit)],
            send_sem=pack_send,
            recv_sem=pack_recv.at[me // 16],
            device_id=(pz * heads + py, mp),
            device_id_type=MESH,
        )

    def send_pack(i, carry):
        pack_copy(i).start()
        return carry

    lax.fori_loop(0, devices - 1, send_pack, 0)
    own_src = pl.multiple_of(y * slots + z * unit, unit)
    own_dst = pl.multiple_of(me * unit, unit)
    pltpu.make_async_copy(
        out_pack.at[pl.ds(own_src, unit)], in_pack.at[pl.ds(own_dst, unit)], pack_recv.at[me // 16]
    ).start()

    after = iota((tok, tok), 0) > iota((tok, tok), 1)
    for h in range(heads):
        b_row = buckets_ref[h : h + 1, :]
        b_col = jnp.sum(jnp.where(eye, b_row, 0), axis=1, keepdims=True)
        rank_col = jnp.sum(jnp.where((b_col == b_row) & after, 1, 0), axis=1, keepdims=True)
        pick_buf[h] = one_hot(iota((tok, slots), 1) == b_col * CAP + rank_col)
    loads[3].wait()
    counts = counts_ref[:, y, :]
    spread = (iota((devices, slots), 1) // CAP) == iota((devices, slots), 0)
    rank = lax.rem(iota((1, slots), 1), CAP)
    dead = []
    for j in range(-1, heads):
        b = lax.rem(z * heads + j + devices, devices)
        column = jnp.sum(jnp.where(iota(counts.shape, 1) == b, counts, 0), axis=1, keepdims=True)
        row = jnp.sum(jnp.where(spread, column, 0), axis=0, keepdims=True)
        dead.append(jnp.where(rank < row, 0.0, DEAD))

    def by_bucket(i):
        return (i // CAP) % 16 * unit + i // part * CAP + i % CAP

    order = one_hot(by_bucket(iota((span, span), 0)) == iota((span, span), 1))
    order_back = one_hot(by_bucket(iota((span, span), 1)) == iota((span, span), 0))

    next_z = lax.rem(z + 1, planes)
    for g in range(groups):
        here = in_pack.at[g * span : (g + 1) * span]
        pltpu.make_async_copy(here, here, pack_recv.at[g]).wait()
        arranged = dot(order, here[...]).astype(BF16)
        rows = slice(g * part, (g + 1) * part)
        for j in range(heads):
            rows_buf[j, rows, :] = arranged[j * part : (j + 1) * part]
        pltpu.make_async_remote_copy(
            src_ref=rows_buf.at[heads - 1, rows],
            dst_ref=prev_buf.at[rows],
            send_sem=next_send,
            recv_sem=next_recv,
            device_id=(next_z * heads + y, mp),
            device_id_type=MESH,
        ).start()

    itself = iota((slots, slots), 0) == iota((slots, slots), 1)
    scale = 1.0 / math.sqrt(dim)

    trans = (((1,), (1,)), ((), ()))

    def own_scores(j):
        q = rows_buf[j, :, :dim]
        own = lax.dot_general(q, q, trans, preferred_element_type=F32)
        return jnp.where(itself, SELF_SCORE, own * scale + dead[j + 1])

    def attend(j, own, prev):
        q = rows_buf[j, :, :dim]
        v = rows_buf[j, :, dim:]
        far = lax.dot_general(q, prev[:, :dim], trans, preferred_element_type=F32) * scale + dead[j]
        top = jnp.maximum(jnp.max(own, axis=1, keepdims=True), jnp.max(far, axis=1, keepdims=True))
        own = jnp.exp(own - top)
        far = jnp.exp(far - top)
        total = jnp.sum(own, axis=1, keepdims=True) + jnp.sum(far, axis=1, keepdims=True)
        share = 1.0 / total
        att = dot((own * share).astype(BF16), v) + dot((far * share).astype(BF16), prev[:, dim:])
        att_buf[j] = att.astype(BF16)

    for j in range(1, heads):
        attend(j, own_scores(j), rows_buf[j - 1])
    own = own_scores(0)
    pltpu.make_async_copy(prev_buf, prev_buf, next_recv).wait()
    attend(0, own, prev_buf[...])

    for g in range(groups):
        rows = slice(g * part, (g + 1) * part)
        mine = jnp.concatenate([att_buf[j, rows, :] for j in range(heads)], axis=0)
        out_ret[g * span : (g + 1) * span, :] = dot(order_back, mine).astype(BF16)

    def ret_copy(i):
        pz, py = peer(i)
        there = pz * heads + py
        return pltpu.make_async_remote_copy(
            src_ref=out_ret.at[pl.ds(pl.multiple_of(there * unit, unit), unit)],
            dst_ref=in_ret.at[pl.ds(own_src, unit)],
            send_sem=ret_send,
            recv_sem=ret_recv.at[y],
            device_id=(there, mp),
            device_id_type=MESH,
        )

    def send_ret(i, carry):
        ret_copy(i).start()
        return carry

    lax.fori_loop(0, devices - 1, send_ret, 0)
    pltpu.make_async_copy(
        out_ret.at[pl.ds(own_dst, unit)], in_ret.at[pl.ds(own_src, unit)], ret_recv.at[y]
    ).start()

    loads[4].wait()
    for h in range(heads):
        here = in_ret.at[h * slots : (h + 1) * slots]
        pltpu.make_async_copy(here, here, ret_recv.at[h]).wait()
        tok_buf[:, h * dim : (h + 1) * dim] = dot(pick_buf[h], here[...]).astype(BF16)

    def share_of(m):
        return dot(tok_buf[...], w_buf[:, pl.ds(pl.multiple_of(m * block, block), block)])

    ways = (2, 1, 3, 0)
    half = tok // 2

    def to_chip(k, src, way):
        cx = lax.rem(x + way, chips)
        copy = pltpu.make_async_remote_copy(
            src_ref=src,
            dst_ref=chip_in.at[k],
            send_sem=chip_send,
            recv_sem=chip_recv.at[k],
            device_id=(me, cx * 2 + core),
            device_id_type=MESH,
        )
        copy.start()

    def give(k):
        cx = lax.rem(x + ways[k], chips)
        pair_out[k] = share_of(cx * 2 + 1 - core).astype(BF16)
        pltpu.make_async_remote_copy(
            src_ref=pair_out.at[k],
            dst_ref=pair_in.at[k],
            send_sem=pair_send,
            recv_sem=pair_recv.at[k],
            device_id=(me, x * 2 + 1 - core),
            device_id_type=MESH,
        ).start()

    def pair_sum(k):
        cx = lax.rem(x + ways[k], chips)
        mine = share_of(cx * 2 + core)
        pltpu.make_async_copy(pair_in.at[k], pair_in.at[k], pair_recv.at[k]).wait()
        return mine + pair_in[k].astype(F32)

    def arrived(k):
        pltpu.make_async_copy(chip_in.at[k], chip_in.at[k], chip_recv.at[k]).wait()
        return chip_in[k].astype(F32)

    def put(k, rows, way):
        chip_out[k] = rows.astype(BF16)
        to_chip(k, chip_out.at[k], way)

    give(0)
    give(1)
    opposite = pair_sum(0)
    put(0, opposite[:half], 1)
    put(1, opposite[half:], 3)
    give(2)
    right = pair_sum(1)
    put(2, right[half:], 1)
    give(3)
    left = pair_sum(2)
    put(3, left[:half], 3)
    put(4, right[:half] + arrived(0), 1)
    put(5, left[half:] + arrived(1), 3)
    total = pair_sum(3)
    upper = total[:half] + arrived(3)
    lower = total[half:] + arrived(2)
    out_ref[:half, :] = (upper + arrived(4)).astype(BF16)
    out_ref[half:, :] = (lower + arrived(5)).astype(BF16)

    most = (devices - 1) * unit
    pltpu.make_async_copy(out_pack.at[:most], out_pack.at[:most], pack_send).wait()
    pltpu.make_async_copy(prev_buf, prev_buf, next_send).wait()
    pltpu.make_async_copy(out_ret.at[:most], out_ret.at[:most], ret_send).wait()
    pltpu.make_async_copy(pair_out, pair_out, pair_send).wait()
    pltpu.make_async_copy(chip_out, chip_out, chip_send).wait()


def local(planes, chips, shared_qk, values, buckets, counts, w_out):
    buckets = buckets.T
    tok, width = shared_qk.shape
    heads = buckets.shape[0]
    dim = width // heads
    devices = planes * heads
    slots = devices * CAP
    groups = devices // 16
    block = w_out.shape[1] // (2 * chips)
    vmem = pl.BlockSpec(memory_space=pltpu.VMEM)
    dma = pltpu.SemaphoreType.DMA
    return pl.pallas_call(
        functools.partial(layer_kernel, planes, heads, chips, tok, dim),
        out_shape=jax.ShapeDtypeStruct((tok, block), BF16),
        in_specs=[pl.BlockSpec(memory_space=pl.ANY)] * 5,
        out_specs=vmem,
        scratch_shapes=[
            pltpu.VMEM(shared_qk.shape, BF16),
            pltpu.VMEM(values.shape, BF16),
            pltpu.VMEM(buckets.shape, jnp.int32),
            pltpu.VMEM(counts.shape, jnp.int32),
            pltpu.VMEM(w_out.shape, BF16),
            pltpu.VMEM((heads * slots, 2 * dim), BF16),
            pltpu.VMEM((heads * slots, 2 * dim), BF16),
            pltpu.VMEM((heads, slots, 2 * dim), BF16),
            pltpu.VMEM((slots, 2 * dim), BF16),
            pltpu.VMEM((heads, slots, dim), BF16),
            pltpu.VMEM((heads * slots, dim), BF16),
            pltpu.VMEM((heads * slots, dim), BF16),
            pltpu.VMEM((tok, heads * dim), BF16),
            pltpu.VMEM((heads, tok, slots), BF16),
            pltpu.VMEM((chips, tok, block), BF16),
            pltpu.VMEM((chips, tok, block), BF16),
            pltpu.VMEM((6, tok // 2, block), BF16),
            pltpu.VMEM((6, tok // 2, block), BF16),
            dma((4,)),
            dma,
            dma,
            dma((groups,)),
            dma,
            dma,
            dma,
            dma((heads,)),
            dma,
            dma((chips,)),
            dma,
            dma((6,)),
        ],
        compiler_params=pltpu.CompilerParams(
            collective_id=0, has_side_effects=True, vmem_limit_bytes=60 * 1024 * 1024
        ),
    )(shared_qk, values, buckets, counts, w_out)


def solution(mesh):
    placed = (P("seq", "mp"), P("seq", "mp"), P("seq", "mp"), P(None, "mp", None), P("mp", None))
    heads = 4
    planes = mesh.shape["seq"] // heads
    chips = mesh.shape["mp"] // 2
    return jax.shard_map(
        functools.partial(local, planes, chips),
        mesh=mesh, in_specs=placed, out_specs=P("seq", "mp"), check_vma=False,
    )
```

```python
import functools
import math

import jax
import jax.numpy as jnp
from jax import lax
from jax.experimental import pallas as pl
from jax.experimental.pallas import tpu as pltpu
from jax.sharding import PartitionSpec as P

CAP = 4
SELF_SCORE = -100000.0
DEAD = -1e30
BF16 = jnp.bfloat16
F32 = jnp.float32
MESH = pl.DeviceIdType.MESH


def iota(shape, dim):
    return lax.broadcasted_iota(jnp.int32, shape, dim)


def one_hot(mask):
    return jnp.where(mask, 1.0, 0.0).astype(BF16)


def dot(a, b):
    return jnp.dot(a, b, preferred_element_type=F32)


def layer_kernel(
    planes, heads, chips, tok, dim,
    qk_hbm, val_hbm, buckets_hbm, counts_hbm, w_hbm, out_ref,
    qk_ref, val_ref, buckets_ref, counts_ref, w_buf, out_pack, in_pack, rows_buf, prev_buf, att_buf, out_ret, in_ret, tok_buf, pick_buf,
    pair_out, pair_in, chip_out, chip_in,
    load_sem, w_sem, pack_send, pack_recv, next_send, next_recv, ret_send, ret_recv,
    pair_send, pair_recv, chip_send, chip_recv,
):
    devices = planes * heads
    slots = devices * CAP
    unit = heads * CAP
    groups = devices // 16
    span = 16 * unit
    part = 16 * CAP
    block = w_hbm.shape[1] // (2 * chips)
    me = lax.axis_index("seq")
    mp = lax.axis_index("mp")
    z, y = me // heads, lax.rem(me, heads)
    x, core = mp // 2, lax.rem(mp, 2)

    loads = [
        pltpu.make_async_copy(buckets_hbm, buckets_ref, load_sem.at[0]),
        pltpu.make_async_copy(qk_hbm, qk_ref, load_sem.at[1]),
        pltpu.make_async_copy(val_hbm, val_ref, load_sem.at[2]),
        pltpu.make_async_copy(counts_hbm, counts_ref, load_sem.at[3]),
        pltpu.make_async_copy(w_hbm, w_buf, w_sem),
    ]
    for load in loads:
        load.start()

    barrier = pltpu.get_barrier_semaphore()

    def greet(k, carry):
        other = lax.rem(me + k, devices)
        pl.semaphore_signal(barrier, inc=1, device_id=(other, mp), device_id_type=MESH)
        return carry

    lax.fori_loop(1, devices, greet, 0)
    pl.semaphore_signal(barrier, inc=1, device_id=(me, x * 2 + 1 - core), device_id_type=MESH)
    for off in range(1, chips):
        there = lax.rem(x + off, chips) * 2 + core
        pl.semaphore_signal(barrier, inc=1, device_id=(me, there), device_id_type=MESH)

    eye = iota((tok, tok), 0) == iota((tok, tok), 1)
    before = iota((tok, tok), 0) < iota((tok, tok), 1)
    out_row = iota((slots, 2 * tok), 0)
    wanted = out_row // unit * unit + out_row % (unit // 2) + out_row // (unit // 2) % 2 * slots
    for load in loads[:3]:
        load.wait()
    for h in range(heads):
        b_row = buckets_ref[h : h + 1, :]
        b_col = jnp.sum(jnp.where(eye, b_row, 0), axis=1, keepdims=True)
        rank_row = jnp.sum(jnp.where((b_col == b_row) & before, 1, 0), axis=0, keepdims=True)
        slot_row = b_row * CAP + rank_row
        slot_row = jnp.concatenate([slot_row, slot_row + slots], axis=1)
        cols = slice(h * dim, (h + 1) * dim)
        tokens = jnp.concatenate([qk_ref[:, cols], val_ref[:, cols]], axis=0)
        for p in range(2):
            place = one_hot(wanted + (unit // 2 if p == 0 else 0) == slot_row)
            out_pack[p, h * slots : (h + 1) * slots, :] = dot(place, tokens).astype(BF16)

    pl.semaphore_wait(barrier, devices - 1 + chips)

    def peer(i):
        a = i // heads
        half = planes // 2
        dz = jnp.where(lax.rem(a, 2) == 1, half - (a + 1) // 2, half + a // 2)
        pz = lax.rem(z + dz, planes)
        py = lax.rem(y + heads - 1 - lax.rem(i, heads), heads)
        return pz, py

    def pack_copy(p, i):
        pz, py = peer(i)
        src = pl.multiple_of(py * slots + pz * unit, unit)
        dst = pl.multiple_of(me * unit, unit)
        return pltpu.make_async_remote_copy(
            src_ref=out_pack.at[p, pl.ds(src, unit)],
            dst_ref=in_pack.at[p, pl.ds(dst, unit)],
            send_sem=pack_send.at[p],
            recv_sem=pack_recv.at[p, me // 16],
            device_id=(pz * heads + py, mp),
            device_id_type=MESH,
        )

    own_src = pl.multiple_of(y * slots + z * unit, unit)
    own_dst = pl.multiple_of(me * unit, unit)
    for p in range(2):
        def send_pack(i, carry, p=p):
            pack_copy(p, i).start()
            return carry

        lax.fori_loop(0, devices - 1, send_pack, 0)
        pltpu.make_async_copy(
            out_pack.at[p, pl.ds(own_src, unit)],
            in_pack.at[p, pl.ds(own_dst, unit)],
            pack_recv.at[p, me // 16],
        ).start()

    after = iota((tok, tok), 0) > iota((tok, tok), 1)
    for h in range(heads):
        b_row = buckets_ref[h : h + 1, :]
        b_col = jnp.sum(jnp.where(eye, b_row, 0), axis=1, keepdims=True)
        rank_col = jnp.sum(jnp.where((b_col == b_row) & after, 1, 0), axis=1, keepdims=True)
        pick_buf[h] = one_hot(iota((tok, slots), 1) == b_col * CAP + rank_col)
    loads[3].wait()
    counts = counts_ref[:, y, :]
    spread = (iota((devices, slots), 1) // CAP) == iota((devices, slots), 0)
    rank = lax.rem(iota((1, slots), 1), CAP)
    dead = []
    for j in range(-1, heads):
        b = lax.rem(z * heads + j + devices, devices)
        column = jnp.sum(jnp.where(iota(counts.shape, 1) == b, counts, 0), axis=1, keepdims=True)
        row = jnp.sum(jnp.where(spread, column, 0), axis=0, keepdims=True)
        dead.append(jnp.where(rank < row, 0.0, DEAD))

    def by_bucket(i):
        return i // CAP % 16 * unit + i // part // 2 * (unit // 2) + i // part % 2 * CAP + i % CAP

    order = one_hot(by_bucket(iota((span, span), 0)) == iota((span, span), 1))

    def by_source(i):
        return i // CAP % 16 * unit + i // part * CAP + i % CAP

    order_back = one_hot(by_source(iota((span, span), 1)) == iota((span, span), 0))

    def receive(p):
        for g in range(groups):
            here = in_pack.at[p, g * span : (g + 1) * span]
            pltpu.make_async_copy(here, here, pack_recv.at[p, g]).wait()
            arranged = dot(order, here[...]).astype(BF16)
            for n in range(4):
                j = n % 2 + (heads // 2 if p == 0 else 0)
                rows_buf[j, n // 2, g * part : (g + 1) * part, :] = arranged[n * part : (n + 1) * part]

    receive(0)
    next_z = lax.rem(z + 1, planes)
    to_next = pltpu.make_async_remote_copy(
        src_ref=rows_buf.at[heads - 1],
        dst_ref=prev_buf,
        send_sem=next_send,
        recv_sem=next_recv,
        device_id=(next_z * heads + y, mp),
        device_id_type=MESH,
    )
    to_next.start()

    scale = 1.0 / math.sqrt(dim)
    trans = (((1,), (1,)), ((), ()))

    def attend(j, prev, first, count):
        rows = slice(first, first + count)
        itself = iota((count, slots), 0) + first == iota((count, slots), 1)
        q = rows_buf[j, 0, rows, :]
        own = lax.dot_general(q, rows_buf[j, 0], trans, preferred_element_type=F32)
        own = jnp.where(itself, SELF_SCORE, own * scale + dead[j + 1])
        far = lax.dot_general(q, prev[0], trans, preferred_element_type=F32) * scale + dead[j]
        top = jnp.maximum(jnp.max(own, axis=1, keepdims=True), jnp.max(far, axis=1, keepdims=True))
        own = jnp.exp(own - top)
        far = jnp.exp(far - top)
        total = jnp.sum(own, axis=1, keepdims=True) + jnp.sum(far, axis=1, keepdims=True)
        share = 1.0 / total
        att = dot((own * share).astype(BF16), rows_buf[j, 1]) + dot((far * share).astype(BF16), prev[1])
        att_buf[j, rows, :] = att.astype(BF16)

    attend(heads - 1, rows_buf.at[heads - 2], 0, slots)
    receive(1)
    to_next.wait_recv()

    def send_ret(c):
        def body(i, carry):
            pz, py = peer(i)
            there = pz * heads + py

            @pl.when(pz // (planes // 2) == c)
            def _():
                pltpu.make_async_remote_copy(
                    src_ref=out_ret.at[pl.ds(pl.multiple_of(there * unit, unit), unit)],
                    dst_ref=in_ret.at[pl.ds(own_src, unit)],
                    send_sem=ret_send,
                    recv_sem=ret_recv.at[y],
                    device_id=(there, mp),
                    device_id_type=MESH,
                ).start()

            return carry

        lax.fori_loop(0, devices - 1, body, 0)

    for c in range(2):
        for j in range(heads - 1):
            attend(j, rows_buf.at[j - 1] if j else prev_buf, c * slots // 2, slots // 2)
        for g in range(c * groups // 2, (c + 1) * groups // 2):
            rows = slice(g * part, (g + 1) * part)
            mine = jnp.concatenate([att_buf[j, rows, :] for j in range(heads)], axis=0)
            out_ret[g * span : (g + 1) * span, :] = dot(order_back, mine).astype(BF16)
        send_ret(c)
    pltpu.make_async_copy(
        out_ret.at[pl.ds(own_dst, unit)], in_ret.at[pl.ds(own_src, unit)], ret_recv.at[y]
    ).start()

    loads[4].wait()
    for h in range(heads):
        here = in_ret.at[h * slots : (h + 1) * slots]
        pltpu.make_async_copy(here, here, ret_recv.at[h]).wait()
        tok_buf[:, h * dim : (h + 1) * dim] = dot(pick_buf[h], here[...]).astype(BF16)

    def share_of(m):
        return dot(tok_buf[...], w_buf[:, pl.ds(pl.multiple_of(m * block, block), block)])

    ways = (2, 1, 3, 0)
    half = tok // 2

    def to_chip(k, src, way):
        cx = lax.rem(x + way, chips)
        copy = pltpu.make_async_remote_copy(
            src_ref=src,
            dst_ref=chip_in.at[k],
            send_sem=chip_send,
            recv_sem=chip_recv.at[k],
            device_id=(me, cx * 2 + core),
            device_id_type=MESH,
        )
        copy.start()

    def give(k):
        cx = lax.rem(x + ways[k], chips)
        pair_out[k] = share_of(cx * 2 + 1 - core).astype(BF16)
        pltpu.make_async_remote_copy(
            src_ref=pair_out.at[k],
            dst_ref=pair_in.at[k],
            send_sem=pair_send,
            recv_sem=pair_recv.at[k],
            device_id=(me, x * 2 + 1 - core),
            device_id_type=MESH,
        ).start()

    def pair_sum(k):
        cx = lax.rem(x + ways[k], chips)
        mine = share_of(cx * 2 + core)
        pltpu.make_async_copy(pair_in.at[k], pair_in.at[k], pair_recv.at[k]).wait()
        return mine + pair_in[k].astype(F32)

    def arrived(k):
        pltpu.make_async_copy(chip_in.at[k], chip_in.at[k], chip_recv.at[k]).wait()
        return chip_in[k].astype(F32)

    def put(k, rows, way):
        chip_out[k] = rows.astype(BF16)
        to_chip(k, chip_out.at[k], way)

    give(0)
    give(1)
    opposite = pair_sum(0)
    put(0, opposite[:half], 1)
    put(1, opposite[half:], 3)
    give(2)
    right = pair_sum(1)
    put(2, right[half:], 1)
    give(3)
    left = pair_sum(2)
    put(3, left[:half], 3)
    put(4, right[:half] + arrived(0), 1)
    put(5, left[half:] + arrived(1), 3)
    total = pair_sum(3)
    upper = total[:half] + arrived(3)
    lower = total[half:] + arrived(2)
    out_ref[:half, :] = (upper + arrived(4)).astype(BF16)
    out_ref[half:, :] = (lower + arrived(5)).astype(BF16)

    most = (devices - 1) * unit
    for p in range(2):
        pltpu.make_async_copy(out_pack.at[p, :most], out_pack.at[p, :most], pack_send.at[p]).wait()
    to_next.wait_send()
    pltpu.make_async_copy(out_ret.at[:most], out_ret.at[:most], ret_send).wait()
    pltpu.make_async_copy(pair_out, pair_out, pair_send).wait()
    pltpu.make_async_copy(chip_out, chip_out, chip_send).wait()


def local(planes, chips, shared_qk, values, buckets, counts, w_out):
    buckets = buckets.T
    tok, width = shared_qk.shape
    heads = buckets.shape[0]
    dim = width // heads
    devices = planes * heads
    slots = devices * CAP
    groups = devices // 16
    block = w_out.shape[1] // (2 * chips)
    vmem = pl.BlockSpec(memory_space=pltpu.VMEM)
    dma = pltpu.SemaphoreType.DMA
    return pl.pallas_call(
        functools.partial(layer_kernel, planes, heads, chips, tok, dim),
        out_shape=jax.ShapeDtypeStruct((tok, block), BF16),
        in_specs=[pl.BlockSpec(memory_space=pl.ANY)] * 5,
        out_specs=vmem,
        scratch_shapes=[
            pltpu.VMEM(shared_qk.shape, BF16),
            pltpu.VMEM(values.shape, BF16),
            pltpu.VMEM(buckets.shape, jnp.int32),
            pltpu.VMEM(counts.shape, jnp.int32),
            pltpu.VMEM(w_out.shape, BF16),
            pltpu.VMEM((2, heads * slots, dim), BF16),
            pltpu.VMEM((2, heads * slots, dim), BF16),
            pltpu.VMEM((heads, 2, slots, dim), BF16),
            pltpu.VMEM((2, slots, dim), BF16),
            pltpu.VMEM((heads, slots, dim), BF16),
            pltpu.VMEM((heads * slots, dim), BF16),
            pltpu.VMEM((heads * slots, dim), BF16),
            pltpu.VMEM((tok, heads * dim), BF16),
            pltpu.VMEM((heads, tok, slots), BF16),
            pltpu.VMEM((chips, tok, block), BF16),
            pltpu.VMEM((chips, tok, block), BF16),
            pltpu.VMEM((6, tok // 2, block), BF16),
            pltpu.VMEM((6, tok // 2, block), BF16),
            dma((4,)),
            dma,
            dma((2,)),
            dma((2, groups)),
            dma,
            dma,
            dma,
            dma((heads,)),
            dma,
            dma((chips,)),
            dma,
            dma((6,)),
        ],
        compiler_params=pltpu.CompilerParams(
            collective_id=0, has_side_effects=True, vmem_limit_bytes=60 * 1024 * 1024
        ),
    )(shared_qk, values, buckets, counts, w_out)


def solution(mesh):
    placed = (P("seq", "mp"), P("seq", "mp"), P("seq", "mp"), P(None, "mp", None), P("mp", None))
    heads = 4
    planes = mesh.shape["seq"] // heads
    chips = mesh.shape["mp"] // 2
    return jax.shard_map(
        functools.partial(local, planes, chips),
        mesh=mesh, in_specs=placed, out_specs=P("seq", "mp"), check_vma=False,
    )
```

```python
import functools
import math

import jax
import jax.numpy as jnp
from jax import lax
from jax.experimental import pallas as pl
from jax.experimental.pallas import tpu as pltpu
from jax.sharding import PartitionSpec as P

CAP = 4
SELF_SCORE = -100000.0
DEAD = -1e30
BF16 = jnp.bfloat16
F32 = jnp.float32
MESH = pl.DeviceIdType.MESH


def iota(shape, dim):
    return lax.broadcasted_iota(jnp.int32, shape, dim)


def one_hot(mask):
    return jnp.where(mask, 1.0, 0.0).astype(BF16)


def dot(a, b):
    return jnp.dot(a, b, preferred_element_type=F32)


def layer_kernel(
    planes, heads, chips, tok, dim,
    qk_hbm, val_hbm, buckets_hbm, counts_hbm, w_hbm, out_ref,
    qk_ref, val_ref, buckets_ref, counts_ref, w_buf, out_pack, in_pack, rows_buf, prev_buf, att_buf, out_ret, in_ret, tok_buf, pick_buf,
    pair_out, pair_in, chip_out, chip_in,
    load_sem, w_sem, pack_send, pack_recv, next_send, next_recv, ret_send, ret_recv,
    pair_send, pair_recv, chip_send, chip_recv, turn,
):
    devices = planes * heads
    slots = devices * CAP
    unit = heads * CAP
    groups = devices // 16
    span = 16 * unit
    part = 16 * CAP
    block = w_hbm.shape[1] // (2 * chips)
    me = lax.axis_index("seq")
    mp = lax.axis_index("mp")
    z, y = me // heads, lax.rem(me, heads)
    x, core = mp // 2, lax.rem(mp, 2)

    loads = [
        pltpu.make_async_copy(buckets_hbm, buckets_ref, load_sem.at[0]),
        pltpu.make_async_copy(qk_hbm, qk_ref, load_sem.at[1]),
        pltpu.make_async_copy(val_hbm, val_ref, load_sem.at[2]),
        pltpu.make_async_copy(counts_hbm, counts_ref, load_sem.at[3]),
        pltpu.make_async_copy(w_hbm, w_buf, w_sem),
    ]
    for load in loads:
        load.start()

    barrier = pltpu.get_barrier_semaphore()

    def wrap(i, n):
        return i - jnp.where(i >= n, n, 0)

    ys = [wrap(y + dy, heads) for dy in range(heads)]

    def group_of(pz):
        return jnp.where(core == 0, pz, wrap(planes - pz, planes))

    group = group_of(z)

    def plane(a):
        half = planes // 2
        return wrap(z + jnp.where(a % 2 == 1, half - (a + 1) // 2, half + a // 2), planes)

    def greet(a, carry):
        pz = plane(a)
        for py in ys:
            pl.semaphore_signal(barrier, inc=1, device_id=(pz * heads + py, mp), device_id_type=MESH)
        return carry

    lax.fori_loop(0, planes - 1, greet, 0)
    for py in ys[1:]:
        pl.semaphore_signal(barrier, inc=1, device_id=(z * heads + py, mp), device_id_type=MESH)
    pl.semaphore_signal(barrier, inc=1, device_id=(me, x * 2 + 1 - core), device_id_type=MESH)
    for off in range(1, chips):
        there = lax.rem(x + off, chips) * 2 + core
        pl.semaphore_signal(barrier, inc=1, device_id=(me, there), device_id_type=MESH)

    eye = iota((tok, tok), 0) == iota((tok, tok), 1)
    before = iota((tok, tok), 0) < iota((tok, tok), 1)
    out_row = iota((slots, 2 * tok), 0)
    wanted = out_row // unit * unit + out_row % (unit // 2) + out_row // (unit // 2) % 2 * slots
    for load in loads[:3]:
        load.wait()
    for h in range(heads):
        b_row = buckets_ref[h : h + 1, :]
        b_col = jnp.sum(jnp.where(eye, b_row, 0), axis=1, keepdims=True)
        rank_row = jnp.sum(jnp.where((b_col == b_row) & before, 1, 0), axis=0, keepdims=True)
        slot_row = b_row * CAP + rank_row
        slot_row = jnp.concatenate([slot_row, slot_row + slots], axis=1)
        cols = slice(h * dim, (h + 1) * dim)
        tokens = jnp.concatenate([qk_ref[:, cols], val_ref[:, cols]], axis=0)
        for p in range(2):
            place = one_hot(wanted + (unit // 2 if p == 0 else 0) == slot_row)
            out_pack[p, h * slots : (h + 1) * slots, :] = dot(place, tokens).astype(BF16)

    pl.semaphore_wait(barrier, devices - 1 + chips)

    def send_pack(p, pz, py):
        src = pl.multiple_of(py * slots + group_of(pz) * unit, unit)
        pltpu.make_async_remote_copy(
            src_ref=out_pack.at[p, pl.ds(src, unit)],
            dst_ref=in_pack.at[p, pl.ds(own_dst, unit)],
            send_sem=pack_send.at[p],
            recv_sem=pack_recv.at[p, me // 16],
            device_id=(pz * heads + py, mp),
            device_id_type=MESH,
        ).start()

    own_src = pl.multiple_of(y * slots + group * unit, unit)
    own_dst = pl.multiple_of(me * unit, unit)
    @pl.when(core != 0)
    def _():
        pl.semaphore_wait(turn, 1)

    for p in range(2):
        def to_plane(a, carry, p=p):
            pz = plane(a)
            for py in ys:
                send_pack(p, pz, py)
            return carry

        lax.fori_loop(0, planes - 1, to_plane, 0)
        for py in ys[1:]:
            send_pack(p, z, py)
        pltpu.make_async_copy(
            out_pack.at[p, pl.ds(own_src, unit)],
            in_pack.at[p, pl.ds(own_dst, unit)],
            pack_recv.at[p, me // 16],
        ).start()

    most = (devices - 1) * unit

    def wait_sent(p):
        pltpu.make_async_copy(out_pack.at[p, :most], out_pack.at[p, :most], pack_send.at[p]).wait()

    @pl.when(core == 0)
    def _():
        wait_sent(0)
        pl.semaphore_signal(turn, inc=1, device_id=(me, x * 2 + 1 - core), device_id_type=MESH)

    after = iota((tok, tok), 0) > iota((tok, tok), 1)
    for h in range(heads):
        b_row = buckets_ref[h : h + 1, :]
        b_col = jnp.sum(jnp.where(eye, b_row, 0), axis=1, keepdims=True)
        rank_col = jnp.sum(jnp.where((b_col == b_row) & after, 1, 0), axis=1, keepdims=True)
        pick_buf[h] = one_hot(iota((tok, slots), 1) == b_col * CAP + rank_col)
    loads[3].wait()
    counts = counts_ref[:, y, :]
    spread = (iota((devices, slots), 1) // CAP) == iota((devices, slots), 0)
    rank = lax.rem(iota((1, slots), 1), CAP)
    dead = []
    for j in range(-1, heads):
        b = lax.rem(group * heads + j + devices, devices)
        column = jnp.sum(jnp.where(iota(counts.shape, 1) == b, counts, 0), axis=1, keepdims=True)
        row = jnp.sum(jnp.where(spread, column, 0), axis=0, keepdims=True)
        dead.append(jnp.where(rank < row, 0.0, DEAD))

    def by_bucket(i):
        return i // CAP % 16 * unit + i // part // 2 * (unit // 2) + i // part % 2 * CAP + i % CAP

    order = one_hot(by_bucket(iota((span, span), 0)) == iota((span, span), 1))

    def by_source(i):
        return i // CAP % 16 * unit + i // part * CAP + i % CAP

    order_back = one_hot(by_source(iota((span, span), 1)) == iota((span, span), 0))

    def receive(p):
        for g in range(groups):
            here = in_pack.at[p, g * span : (g + 1) * span]
            pltpu.make_async_copy(here, here, pack_recv.at[p, g]).wait()
            arranged = dot(order, here[...]).astype(BF16)
            for n in range(4):
                j = n % 2 + (heads // 2 if p == 0 else 0)
                rows_buf[j, n // 2, g * part : (g + 1) * part, :] = arranged[n * part : (n + 1) * part]

    receive(0)
    next_z = wrap(z + jnp.where(core == 0, 1, planes - 1), planes)
    to_next = pltpu.make_async_remote_copy(
        src_ref=rows_buf.at[heads - 1],
        dst_ref=prev_buf,
        send_sem=next_send,
        recv_sem=next_recv,
        device_id=(next_z * heads + y, mp),
        device_id_type=MESH,
    )
    to_next.start()

    scale = 1.0 / math.sqrt(dim)
    trans = (((1,), (1,)), ((), ()))

    def attend(j, prev, first, count):
        rows = slice(first, first + count)
        itself = iota((count, slots), 0) + first == iota((count, slots), 1)
        q = rows_buf[j, 0, rows, :]
        own = lax.dot_general(q, rows_buf[j, 0], trans, preferred_element_type=F32)
        own = jnp.where(itself, SELF_SCORE, own * scale + dead[j + 1])
        far = lax.dot_general(q, prev[0], trans, preferred_element_type=F32) * scale + dead[j]
        top = jnp.maximum(jnp.max(own, axis=1, keepdims=True), jnp.max(far, axis=1, keepdims=True))
        own = jnp.exp(own - top)
        far = jnp.exp(far - top)
        total = jnp.sum(own, axis=1, keepdims=True) + jnp.sum(far, axis=1, keepdims=True)
        share = 1.0 / total
        att = dot((own * share).astype(BF16), rows_buf[j, 1]) + dot((far * share).astype(BF16), prev[1])
        att_buf[j, rows, :] = att.astype(BF16)

    attend(heads - 1, rows_buf.at[heads - 2], 0, slots)
    receive(1)
    to_next.wait_recv()

    def send_ret(c, pz, py):
        there = pz * heads + py
        pltpu.make_async_remote_copy(
            src_ref=out_ret.at[pl.ds(pl.multiple_of(there * unit, unit), unit)],
            dst_ref=in_ret.at[pl.ds(own_src, unit)],
            send_sem=ret_send.at[c],
            recv_sem=ret_recv.at[y],
            device_id=(there, mp),
            device_id_type=MESH,
        ).start()

    def send_half(c):
        def to_plane(a, carry):
            pz = plane(a)

            @pl.when((pz < 4) == (c == 0))
            def _():
                for py in ys:
                    send_ret(c, pz, py)

            return carry

        lax.fori_loop(0, planes - 1, to_plane, 0)

    for c, (lo, hi) in enumerate(((0, 1), (1, 4))):
        for j in range(heads - 1):
            attend(j, rows_buf.at[j - 1] if j else prev_buf, lo * part, (hi - lo) * part)
        for g in range(lo, hi):
            rows = slice(g * part, (g + 1) * part)
            mine = jnp.concatenate([att_buf[j, rows, :] for j in range(heads)], axis=0)
            out_ret[g * span : (g + 1) * span, :] = dot(order_back, mine).astype(BF16)
        send_half(c)
        @pl.when((z < 4) == (c == 0))
        def _():
            for py in ys[1:]:
                send_ret(c, z, py)
        if c == 0 and False:
            @pl.when(z < 4)
            def _():
                here = out_ret.at[: (4 * heads - 1) * unit]
                pltpu.make_async_copy(here, here, ret_send.at[0]).wait()
            @pl.when(z >= 4)
            def _():
                here = out_ret.at[: 4 * heads * unit]
                pltpu.make_async_copy(here, here, ret_send.at[0]).wait()
    pltpu.make_async_copy(
        out_ret.at[pl.ds(own_dst, unit)], in_ret.at[pl.ds(own_src, unit)], ret_recv.at[y]
    ).start()

    loads[4].wait()
    for h in range(heads):
        here = in_ret.at[h * slots : (h + 1) * slots]
        pltpu.make_async_copy(here, here, ret_recv.at[h]).wait()
        tok_buf[:, h * dim : (h + 1) * dim] = dot(pick_buf[h], here[...]).astype(BF16)

    def share_of(m):
        return dot(tok_buf[...], w_buf[:, pl.ds(pl.multiple_of(m * block, block), block)])

    ways = (2, 1, 3, 0)
    quarter = tok // 4

    def give(k):
        cx = lax.rem(x + ways[k], chips)
        pair_out[k] = share_of(cx * 2 + 1 - core).astype(BF16)
        pltpu.make_async_remote_copy(
            src_ref=pair_out.at[k],
            dst_ref=pair_in.at[k],
            send_sem=pair_send,
            recv_sem=pair_recv.at[k],
            device_id=(me, x * 2 + 1 - core),
            device_id_type=MESH,
        ).start()

    def pair_sum(k):
        cx = lax.rem(x + ways[k], chips)
        mine = share_of(cx * 2 + core)
        pltpu.make_async_copy(pair_in.at[k], pair_in.at[k], pair_recv.at[k]).wait()
        return mine + pair_in[k].astype(F32)

    def put(first, rows, way):
        count = rows.shape[0] // quarter
        here = slice(first, first + count)
        chip_out[here] = rows.astype(BF16).reshape(count, quarter, block)
        pltpu.make_async_remote_copy(
            src_ref=chip_out.at[here],
            dst_ref=chip_in.at[here],
            send_sem=chip_send,
            recv_sem=chip_recv.at[first],
            device_id=(me, lax.rem(x + way, chips) * 2 + core),
            device_id_type=MESH,
        ).start()

    def wait_chip(first, count):
        here = chip_in.at[first : first + count]
        pltpu.make_async_copy(here, here, chip_recv.at[first]).wait()

    def part_of(rows, q):
        return rows[q * quarter : (q + 1) * quarter]

    give(0)
    give(1)
    opposite = pair_sum(0)
    for q in (0, 2, 1, 3):
        put(q, part_of(opposite, q), 1 if q < 2 else 3)
    give(2)
    right = pair_sum(1)
    put(4, right[2 * quarter :], 1)
    give(3)
    left = pair_sum(2)
    put(6, left[: 2 * quarter], 3)
    for q in (0, 2, 1, 3):
        wait_chip(q, 1)
        put(8 + q, part_of(right if q < 2 else left, q) + chip_in[q].astype(F32), 1 if q < 2 else 3)
    total = pair_sum(3)
    wait_chip(4, 2)
    wait_chip(6, 2)
    for q in (0, 2, 1, 3):
        near = part_of(total, q) + chip_in[(6, 7, 4, 5)[q]].astype(F32)
        wait_chip(8 + q, 1)
        out_ref[q * quarter : (q + 1) * quarter, :] = (near + chip_in[8 + q].astype(F32)).astype(BF16)

    @pl.when(core != 0)
    def _():
        wait_sent(0)

    wait_sent(1)
    to_next.wait_send()
    @pl.when(z < 4)
    def _():
        here = out_ret.at[: (4 * heads - 1) * unit]
        pltpu.make_async_copy(here, here, ret_send.at[0]).wait()
    @pl.when(z >= 4)
    def _():
        here = out_ret.at[: 4 * heads * unit]
        pltpu.make_async_copy(here, here, ret_send.at[0]).wait()
    @pl.when(z >= 4)
    def _():
        here = out_ret.at[: (12 * heads - 1) * unit]
        pltpu.make_async_copy(here, here, ret_send.at[1]).wait()
    @pl.when(z < 4)
    def _():
        here = out_ret.at[: 12 * heads * unit]
        pltpu.make_async_copy(here, here, ret_send.at[1]).wait()
    pltpu.make_async_copy(pair_out, pair_out, pair_send).wait()
    pltpu.make_async_copy(chip_out, chip_out, chip_send).wait()


def local(planes, chips, shared_qk, values, buckets, counts, w_out):
    buckets = buckets.T
    tok, width = shared_qk.shape
    heads = buckets.shape[0]
    dim = width // heads
    devices = planes * heads
    slots = devices * CAP
    groups = devices // 16
    block = w_out.shape[1] // (2 * chips)
    vmem = pl.BlockSpec(memory_space=pltpu.VMEM)
    dma = pltpu.SemaphoreType.DMA
    return pl.pallas_call(
        functools.partial(layer_kernel, planes, heads, chips, tok, dim),
        out_shape=jax.ShapeDtypeStruct((tok, block), BF16),
        in_specs=[pl.BlockSpec(memory_space=pl.ANY)] * 5,
        out_specs=vmem,
        scratch_shapes=[
            pltpu.VMEM(shared_qk.shape, BF16),
            pltpu.VMEM(values.shape, BF16),
            pltpu.VMEM(buckets.shape, jnp.int32),
            pltpu.VMEM(counts.shape, jnp.int32),
            pltpu.VMEM(w_out.shape, BF16),
            pltpu.VMEM((2, heads * slots, dim), BF16),
            pltpu.VMEM((2, heads * slots, dim), BF16),
            pltpu.VMEM((heads, 2, slots, dim), BF16),
            pltpu.VMEM((2, slots, dim), BF16),
            pltpu.VMEM((heads, slots, dim), BF16),
            pltpu.VMEM((heads * slots, dim), BF16),
            pltpu.VMEM((heads * slots, dim), BF16),
            pltpu.VMEM((tok, heads * dim), BF16),
            pltpu.VMEM((heads, tok, slots), BF16),
            pltpu.VMEM((chips, tok, block), BF16),
            pltpu.VMEM((chips, tok, block), BF16),
            pltpu.VMEM((12, tok // 4, block), BF16),
            pltpu.VMEM((12, tok // 4, block), BF16),
            dma((4,)),
            dma,
            dma((2,)),
            dma((2, groups)),
            dma,
            dma,
            dma((2,)),
            dma((heads,)),
            dma,
            dma((chips,)),
            dma,
            dma((12,)),
            pltpu.SemaphoreType.REGULAR,
        ],
        compiler_params=pltpu.CompilerParams(
            collective_id=0, has_side_effects=True, vmem_limit_bytes=60 * 1024 * 1024
        ),
    )(shared_qk, values, buckets, counts, w_out)


def solution(mesh):
    placed = (P("seq", "mp"), P("seq", "mp"), P("seq", "mp"), P(None, "mp", None), P("mp", None))
    heads = 4
    planes = mesh.shape["seq"] // heads
    chips = mesh.shape["mp"] // 2
    return jax.shard_map(
        functools.partial(local, planes, chips),
        mesh=mesh, in_specs=placed, out_specs=P("seq", "mp"), check_vma=False,
    )
```

```python
import functools
import math

import jax
import jax.numpy as jnp
from jax import lax
from jax.experimental import pallas as pl
from jax.experimental.pallas import tpu as pltpu
from jax.sharding import PartitionSpec as P

CAP = 4
SELF_SCORE = -100000.0
DEAD = -1e30
LOG2E = math.log2(math.e)
BF16 = jnp.bfloat16
F32 = jnp.float32
MESH = pl.DeviceIdType.MESH


def iota(shape, dim):
    return lax.broadcasted_iota(jnp.int32, shape, dim)


def one_hot(mask):
    return jnp.where(mask, 1.0, 0.0).astype(BF16)


def dot(a, b):
    return jnp.dot(a, b, preferred_element_type=F32)


def layer_kernel(
    planes, heads, chips, tok, dim,
    qk_hbm, val_hbm, buckets_hbm, counts_hbm, w_hbm, out_ref,
    qk_ref, val_ref, buckets_ref, counts_ref, w_buf, out_pack, in_pack, rows_buf, prev_buf, att_buf, out_ret, in_ret, tok_buf, pick_buf,
    pair_out, pair_in, chip_out, chip_in,
    load_sem, w_sem, pack_send, pack_recv, next_send, next_recv, ret_send, ret_recv,
    pair_send, pair_recv, chip_send, chip_recv, turn,
):
    devices = planes * heads
    slots = devices * CAP
    unit = heads * CAP
    groups = devices // 16
    span = 16 * unit
    part = 16 * CAP
    block = w_hbm.shape[1] // (2 * chips)
    me = lax.axis_index("seq")
    mp = lax.axis_index("mp")
    z, y = me // heads, lax.rem(me, heads)
    x, core = mp // 2, lax.rem(mp, 2)

    loads = [
        pltpu.make_async_copy(buckets_hbm, buckets_ref, load_sem.at[0]),
        pltpu.make_async_copy(qk_hbm, qk_ref, load_sem.at[1]),
        pltpu.make_async_copy(val_hbm, val_ref, load_sem.at[2]),
        pltpu.make_async_copy(counts_hbm, counts_ref, load_sem.at[3]),
        pltpu.make_async_copy(w_hbm, w_buf, w_sem),
    ]
    for load in loads:
        load.start()

    barrier = pltpu.get_barrier_semaphore()

    def wrap(i, n):
        return i - jnp.where(i >= n, n, 0)

    ys = [wrap(y + dy, heads) for dy in range(heads)]

    def group_of(pz):
        return jnp.where(core == 0, pz, wrap(planes - pz, planes))

    group = group_of(z)

    def plane(a):
        half = planes // 2
        return wrap(z + jnp.where(a % 2 == 1, half - (a + 1) // 2, half + a // 2), planes)

    def greet(a, carry):
        pz = plane(a)
        for py in ys:
            pl.semaphore_signal(barrier, inc=1, device_id=(pz * heads + py, mp), device_id_type=MESH)
        return carry

    lax.fori_loop(0, planes - 1, greet, 0)
    for py in ys[1:]:
        pl.semaphore_signal(barrier, inc=1, device_id=(z * heads + py, mp), device_id_type=MESH)
    pl.semaphore_signal(barrier, inc=1, device_id=(me, x * 2 + 1 - core), device_id_type=MESH)
    for off in range(1, chips):
        there = lax.rem(x + off, chips) * 2 + core
        pl.semaphore_signal(barrier, inc=1, device_id=(me, there), device_id_type=MESH)

    eye = iota((tok, tok), 0) == iota((tok, tok), 1)
    before = iota((tok, tok), 0) < iota((tok, tok), 1)
    out_row = iota((slots, 2 * tok), 0)
    wanted = out_row // unit * unit + out_row % (unit // 2) + out_row // (unit // 2) % 2 * slots
    for load in loads[:3]:
        load.wait()
    for h in range(heads):
        b_row = buckets_ref[h : h + 1, :]
        b_col = jnp.sum(jnp.where(eye, b_row, 0), axis=1, keepdims=True)
        rank_row = jnp.sum(jnp.where((b_col == b_row) & before, 1, 0), axis=0, keepdims=True)
        slot_row = b_row * CAP + rank_row
        slot_row = jnp.concatenate([slot_row, slot_row + slots], axis=1)
        cols = slice(h * dim, (h + 1) * dim)
        tokens = jnp.concatenate([qk_ref[:, cols], val_ref[:, cols]], axis=0)
        for p in range(2):
            place = one_hot(wanted + (unit // 2 if p == 0 else 0) == slot_row)
            out_pack[p, h * slots : (h + 1) * slots, :] = dot(place, tokens).astype(BF16)

    pl.semaphore_wait(barrier, devices - 1 + chips)

    def send_pack(p, pz, py):
        src = pl.multiple_of(py * slots + group_of(pz) * unit, unit)
        pltpu.make_async_remote_copy(
            src_ref=out_pack.at[p, pl.ds(src, unit)],
            dst_ref=in_pack.at[p, pl.ds(own_dst, unit)],
            send_sem=pack_send.at[p],
            recv_sem=pack_recv.at[p, me // 16],
            device_id=(pz * heads + py, mp),
            device_id_type=MESH,
        ).start()

    own_src = pl.multiple_of(y * slots + group * unit, unit)
    own_dst = pl.multiple_of(me * unit, unit)
    for p in range(2):
        if p == 1:
            @pl.when(core != 0)
            def _():
                pl.semaphore_wait(turn, 1)

        def to_plane(a, carry, p=p):
            pz = plane(a)
            for py in ys:
                send_pack(p, pz, py)
            return carry

        lax.fori_loop(0, planes - 1, to_plane, 0)
        for py in ys[1:]:
            send_pack(p, z, py)
        pltpu.make_async_copy(
            out_pack.at[p, pl.ds(own_src, unit)],
            in_pack.at[p, pl.ds(own_dst, unit)],
            pack_recv.at[p, me // 16],
        ).start()

    most = (devices - 1) * unit

    def wait_sent(p):
        pltpu.make_async_copy(out_pack.at[p, :most], out_pack.at[p, :most], pack_send.at[p]).wait()

    @pl.when(core == 0)
    def _():
        wait_sent(1)
        pl.semaphore_signal(turn, inc=1, device_id=(me, x * 2 + 1 - core), device_id_type=MESH)

    after = iota((tok, tok), 0) > iota((tok, tok), 1)
    for h in range(heads):
        b_row = buckets_ref[h : h + 1, :]
        b_col = jnp.sum(jnp.where(eye, b_row, 0), axis=1, keepdims=True)
        rank_col = jnp.sum(jnp.where((b_col == b_row) & after, 1, 0), axis=1, keepdims=True)
        pick_buf[h] = one_hot(iota((tok, slots), 1) == b_col * CAP + rank_col)
    loads[3].wait()
    counts = counts_ref[:, y, :]
    spread = (iota((devices, slots), 1) // CAP) == iota((devices, slots), 0)
    rank = lax.rem(iota((1, slots), 1), CAP)
    dead = []
    for j in range(-1, heads):
        b = lax.rem(group * heads + j + devices, devices)
        column = jnp.sum(jnp.where(iota(counts.shape, 1) == b, counts, 0), axis=1, keepdims=True)
        row = jnp.sum(jnp.where(spread, column, 0), axis=0, keepdims=True)
        dead.append(jnp.where(rank < row, 0.0, DEAD))

    def by_bucket(i):
        return i // CAP % 16 * unit + i // part // 2 * (unit // 2) + i // part % 2 * CAP + i % CAP

    order = one_hot(by_bucket(iota((span, span), 0)) == iota((span, span), 1))

    def by_source(i):
        return i // CAP % 16 * unit + i // part * CAP + i % CAP

    order_back = one_hot(by_source(iota((span, span), 1)) == iota((span, span), 0))

    def receive(p):
        for g in range(groups):
            here = in_pack.at[p, g * span : (g + 1) * span]
            pltpu.make_async_copy(here, here, pack_recv.at[p, g]).wait()
            arranged = dot(order, here[...]).astype(BF16)
            for n in range(4):
                j = n % 2 + (heads // 2 if p == 0 else 0)
                rows_buf[j, n // 2, g * part : (g + 1) * part, :] = arranged[n * part : (n + 1) * part]

    receive(0)
    next_z = wrap(z + jnp.where(core == 0, 1, planes - 1), planes)
    to_next = pltpu.make_async_remote_copy(
        src_ref=rows_buf.at[heads - 1],
        dst_ref=prev_buf,
        send_sem=next_send,
        recv_sem=next_recv,
        device_id=(next_z * heads + y, mp),
        device_id_type=MESH,
    )
    to_next.start()

    scale = 1.0 / math.sqrt(dim)
    trans = (((1,), (1,)), ((), ()))

    def attend(j, prev, first, count):
        rows = slice(first, first + count)
        itself = iota((count, slots), 0) + first == iota((count, slots), 1)
        q = rows_buf[j, 0, rows, :]
        own = lax.dot_general(q, rows_buf[j, 0], trans, preferred_element_type=F32) + dead[j + 1]
        own = jnp.where(itself, SELF_SCORE / scale, own)
        far = lax.dot_general(q, prev[0], trans, preferred_element_type=F32) + dead[j]
        top = jnp.maximum(jnp.max(own, axis=1, keepdims=True), jnp.max(far, axis=1, keepdims=True))
        own = jnp.exp2((own - top) * (scale * LOG2E))
        far = jnp.exp2((far - top) * (scale * LOG2E))
        share = 1.0 / (jnp.sum(own, axis=1, keepdims=True) + jnp.sum(far, axis=1, keepdims=True))
        att = dot((own * share).astype(BF16), rows_buf[j, 1]) + dot((far * share).astype(BF16), prev[1])
        att_buf[j, rows, :] = att.astype(BF16)

    attend(heads - 1, rows_buf.at[heads - 2], 0, slots)
    receive(1)

    def send_ret(c, pz, py):
        there = pz * heads + py
        pltpu.make_async_remote_copy(
            src_ref=out_ret.at[pl.ds(pl.multiple_of(there * unit, unit), unit)],
            dst_ref=in_ret.at[pl.ds(own_src, unit)],
            send_sem=ret_send.at[c],
            recv_sem=ret_recv.at[y],
            device_id=(there, mp),
            device_id_type=MESH,
        ).start()

    def send_rest():
        def to_plane(a, carry):
            pz = plane(a)

            @pl.when(pz >= 8)
            def _():
                for py in ys:
                    send_ret(1, pz, py)

            return carry

        lax.fori_loop(0, planes - 1, to_plane, 0)

    for c, (lo, hi) in enumerate(((0, 1), (1, 4))):
        for j in (*range(1, heads - 1), 0):
            if j == 0 and c == 0:
                to_next.wait_recv()
            attend(j, rows_buf.at[j - 1] if j else prev_buf, lo * part, (hi - lo) * part)
        for g in range(lo, hi):
            rows = slice(g * part, (g + 1) * part)
            mine = jnp.concatenate([att_buf[j, rows, :] for j in range(heads)], axis=0)
            out_ret[g * span : (g + 1) * span, :] = dot(order_back, mine).astype(BF16)
        if c == 0:
            for pz in range(4):
                @pl.when(z != pz)
                def _(pz=pz):
                    for py in ys:
                        send_ret(c, pz, py)
        else:
            for pz in range(4, 8):
                @pl.when(z != pz)
                def _(pz=pz):
                    for py in ys:
                        send_ret(c, pz, py)
            send_rest()

        @pl.when((z < 4) == (c == 0))
        def _():
            for py in ys[1:]:
                send_ret(c, z, py)

    pltpu.make_async_copy(
        out_ret.at[pl.ds(own_dst, unit)], in_ret.at[pl.ds(own_src, unit)], ret_recv.at[y]
    ).start()

    loads[4].wait()
    for h in range(heads):
        here = in_ret.at[h * slots : (h + 1) * slots]
        pltpu.make_async_copy(here, here, ret_recv.at[h]).wait()
        tok_buf[:, h * dim : (h + 1) * dim] = dot(pick_buf[h], here[...]).astype(BF16)

    def share_of(m):
        return dot(tok_buf[...], w_buf[:, pl.ds(pl.multiple_of(m * block, block), block)])

    ways = (2, 1, 3, 0)
    quarter = tok // 4

    def give(k):
        cx = lax.rem(x + ways[k], chips)
        pair_out[k] = share_of(cx * 2 + 1 - core).astype(BF16)
        pltpu.make_async_remote_copy(
            src_ref=pair_out.at[k],
            dst_ref=pair_in.at[k],
            send_sem=pair_send,
            recv_sem=pair_recv.at[k],
            device_id=(me, x * 2 + 1 - core),
            device_id_type=MESH,
        ).start()

    def pair_sum(k):
        cx = lax.rem(x + ways[k], chips)
        mine = share_of(cx * 2 + core)
        pltpu.make_async_copy(pair_in.at[k], pair_in.at[k], pair_recv.at[k]).wait()
        return mine + pair_in[k].astype(F32)

    def put(first, rows, way):
        count = rows.shape[0] // quarter
        here = slice(first, first + count)
        chip_out[here] = rows.astype(BF16).reshape(count, quarter, block)
        pltpu.make_async_remote_copy(
            src_ref=chip_out.at[here],
            dst_ref=chip_in.at[here],
            send_sem=chip_send,
            recv_sem=chip_recv.at[first],
            device_id=(me, lax.rem(x + way, chips) * 2 + core),
            device_id_type=MESH,
        ).start()

    def wait_chip(first, count):
        here = chip_in.at[first : first + count]
        pltpu.make_async_copy(here, here, chip_recv.at[first]).wait()

    def part_of(rows, q):
        return rows[q * quarter : (q + 1) * quarter]

    give(0)
    give(1)
    opposite = pair_sum(0)
    for q in (0, 2, 1, 3):
        put(q, part_of(opposite, q), 1 if q < 2 else 3)
    give(2)
    right = pair_sum(1)
    put(4, right[2 * quarter :], 1)
    give(3)
    left = pair_sum(2)
    put(6, left[: 2 * quarter], 3)
    for q in (0, 2, 1, 3):
        wait_chip(q, 1)
        put(8 + q, part_of(right if q < 2 else left, q) + chip_in[q].astype(F32), 1 if q < 2 else 3)
    total = pair_sum(3)
    wait_chip(4, 2)
    wait_chip(6, 2)
    for q in (0, 2, 1, 3):
        near = part_of(total, q) + chip_in[(6, 7, 4, 5)[q]].astype(F32)
        wait_chip(8 + q, 1)
        out_ref[q * quarter : (q + 1) * quarter, :] = (near + chip_in[8 + q].astype(F32)).astype(BF16)

    @pl.when(core != 0)
    def _():
        wait_sent(1)

    wait_sent(0)
    to_next.wait_send()
    @pl.when(z < 4)
    def _():
        here = out_ret.at[: (4 * heads - 1) * unit]
        pltpu.make_async_copy(here, here, ret_send.at[0]).wait()
    @pl.when(z >= 4)
    def _():
        here = out_ret.at[: 4 * heads * unit]
        pltpu.make_async_copy(here, here, ret_send.at[0]).wait()
    @pl.when(z >= 4)
    def _():
        here = out_ret.at[: (12 * heads - 1) * unit]
        pltpu.make_async_copy(here, here, ret_send.at[1]).wait()
    @pl.when(z < 4)
    def _():
        here = out_ret.at[: 12 * heads * unit]
        pltpu.make_async_copy(here, here, ret_send.at[1]).wait()
    pltpu.make_async_copy(pair_out, pair_out, pair_send).wait()
    pltpu.make_async_copy(chip_out, chip_out, chip_send).wait()


def local(planes, chips, shared_qk, values, buckets, counts, w_out):
    buckets = buckets.T
    tok, width = shared_qk.shape
    heads = buckets.shape[0]
    dim = width // heads
    devices = planes * heads
    slots = devices * CAP
    groups = devices // 16
    block = w_out.shape[1] // (2 * chips)
    vmem = pl.BlockSpec(memory_space=pltpu.VMEM)
    dma = pltpu.SemaphoreType.DMA
    return pl.pallas_call(
        functools.partial(layer_kernel, planes, heads, chips, tok, dim),
        out_shape=jax.ShapeDtypeStruct((tok, block), BF16),
        in_specs=[pl.BlockSpec(memory_space=pl.ANY)] * 5,
        out_specs=vmem,
        scratch_shapes=[
            pltpu.VMEM(shared_qk.shape, BF16),
            pltpu.VMEM(values.shape, BF16),
            pltpu.VMEM(buckets.shape, jnp.int32),
            pltpu.VMEM(counts.shape, jnp.int32),
            pltpu.VMEM(w_out.shape, BF16),
            pltpu.VMEM((2, heads * slots, dim), BF16),
            pltpu.VMEM((2, heads * slots, dim), BF16),
            pltpu.VMEM((heads, 2, slots, dim), BF16),
            pltpu.VMEM((2, slots, dim), BF16),
            pltpu.VMEM((heads, slots, dim), BF16),
            pltpu.VMEM((heads * slots, dim), BF16),
            pltpu.VMEM((heads * slots, dim), BF16),
            pltpu.VMEM((tok, heads * dim), BF16),
            pltpu.VMEM((heads, tok, slots), BF16),
            pltpu.VMEM((chips, tok, block), BF16),
            pltpu.VMEM((chips, tok, block), BF16),
            pltpu.VMEM((12, tok // 4, block), BF16),
            pltpu.VMEM((12, tok // 4, block), BF16),
            dma((4,)),
            dma,
            dma((2,)),
            dma((2, groups)),
            dma,
            dma,
            dma((2,)),
            dma((heads,)),
            dma,
            dma((chips,)),
            dma,
            dma((12,)),
            pltpu.SemaphoreType.REGULAR,
        ],
        compiler_params=pltpu.CompilerParams(
            collective_id=0, has_side_effects=True, vmem_limit_bytes=60 * 1024 * 1024
        ),
    )(shared_qk, values, buckets, counts, w_out)


def solution(mesh):
    placed = (P("seq", "mp"), P("seq", "mp"), P("seq", "mp"), P(None, "mp", None), P("mp", None))
    heads = 4
    planes = mesh.shape["seq"] // heads
    chips = mesh.shape["mp"] // 2
    return jax.shard_map(
        functools.partial(local, planes, chips),
        mesh=mesh, in_specs=placed, out_specs=P("seq", "mp"), check_vma=False,
    )
```

```python
import functools
import math

import jax
import jax.numpy as jnp
from jax import lax
from jax.experimental import pallas as pl
from jax.experimental.pallas import tpu as pltpu
from jax.sharding import PartitionSpec as P

CAP = 4
SELF_SCORE = -100000.0
DEAD = -1e30
LOG2E = math.log2(math.e)
BF16 = jnp.bfloat16
F32 = jnp.float32
MESH = pl.DeviceIdType.MESH


def iota(shape, dim):
    return lax.broadcasted_iota(jnp.int32, shape, dim)


def one_hot(mask):
    return jnp.where(mask, 1.0, 0.0).astype(BF16)


def dot(a, b):
    return jnp.dot(a, b, preferred_element_type=F32)


def layer_kernel(
    planes, heads, chips, tok, dim,
    qk_hbm, val_hbm, buckets_hbm, counts_hbm, w_hbm, out_ref,
    qk_ref, val_ref, buckets_ref, counts_ref, w_buf, out_pack, in_pack, rows_buf, prev_buf, att_buf, out_ret, in_ret, tok_buf, pick_buf,
    pair_out, pair_in, chip_out, chip_in,
    load_sem, w_sem, pack_send, pack_recv, next_send, next_recv, ret_send, ret_recv,
    pair_send, pair_recv, chip_send, chip_recv, turn,
):
    devices = planes * heads
    slots = devices * CAP
    unit = heads * CAP
    groups = devices // 16
    span = 16 * unit
    part = 16 * CAP
    block = w_hbm.shape[1] // (2 * chips)
    me = lax.axis_index("seq")
    mp = lax.axis_index("mp")
    z, y = me // heads, lax.rem(me, heads)
    x, core = mp // 2, lax.rem(mp, 2)

    loads = [
        pltpu.make_async_copy(buckets_hbm, buckets_ref, load_sem.at[0]),
        pltpu.make_async_copy(qk_hbm, qk_ref, load_sem.at[1]),
        pltpu.make_async_copy(val_hbm, val_ref, load_sem.at[2]),
        pltpu.make_async_copy(counts_hbm, counts_ref, load_sem.at[3]),
        pltpu.make_async_copy(w_hbm, w_buf, w_sem),
    ]
    for load in loads:
        load.start()

    barrier = pltpu.get_barrier_semaphore()

    def wrap(i, n):
        return i - jnp.where(i >= n, n, 0)

    ys = [wrap(y + dy, heads) for dy in range(heads)]

    def group_of(pz):
        return jnp.where(core == 0, pz, wrap(planes - pz, planes))

    group = group_of(z)

    def plane(a):
        half = planes // 2
        return wrap(z + jnp.where(a % 2 == 1, half - (a + 1) // 2, half + a // 2), planes)

    def greet(a, carry):
        pz = plane(a)
        for py in ys:
            pl.semaphore_signal(barrier, inc=1, device_id=(pz * heads + py, mp), device_id_type=MESH)
        return carry

    lax.fori_loop(0, planes - 1, greet, 0)
    for py in ys[1:]:
        pl.semaphore_signal(barrier, inc=1, device_id=(z * heads + py, mp), device_id_type=MESH)
    pl.semaphore_signal(barrier, inc=1, device_id=(me, x * 2 + 1 - core), device_id_type=MESH)
    for off in range(1, chips):
        there = lax.rem(x + off, chips) * 2 + core
        pl.semaphore_signal(barrier, inc=1, device_id=(me, there), device_id_type=MESH)

    eye = iota((tok, tok), 0) == iota((tok, tok), 1)
    before = iota((tok, tok), 0) < iota((tok, tok), 1)
    out_row = iota((slots, 2 * tok), 0)
    wanted = out_row // unit * unit + out_row % (unit // 2) + out_row // (unit // 2) % 2 * slots
    for load in loads[:3]:
        load.wait()
    for h in range(heads):
        b_row = buckets_ref[h : h + 1, :]
        b_col = jnp.sum(jnp.where(eye, b_row, 0), axis=1, keepdims=True)
        rank_row = jnp.sum(jnp.where((b_col == b_row) & before, 1, 0), axis=0, keepdims=True)
        slot_row = b_row * CAP + rank_row
        slot_row = jnp.concatenate([slot_row, slot_row + slots], axis=1)
        cols = slice(h * dim, (h + 1) * dim)
        tokens = jnp.concatenate([qk_ref[:, cols], val_ref[:, cols]], axis=0)
        for p in range(2):
            place = one_hot(wanted + (unit // 2 if p == 0 else 0) == slot_row)
            out_pack[p, h * slots : (h + 1) * slots, :] = dot(place, tokens).astype(BF16)

    pl.semaphore_wait(barrier, devices - 1 + chips)

    def send_pack(p, pz, py):
        src = pl.multiple_of(py * slots + group_of(pz) * unit, unit)
        pltpu.make_async_remote_copy(
            src_ref=out_pack.at[p, pl.ds(src, unit)],
            dst_ref=in_pack.at[p, pl.ds(own_dst, unit)],
            send_sem=pack_send.at[p],
            recv_sem=pack_recv.at[p, me // 16],
            device_id=(pz * heads + py, mp),
            device_id_type=MESH,
        ).start()

    own_src = pl.multiple_of(y * slots + group * unit, unit)
    own_dst = pl.multiple_of(me * unit, unit)
    for p in range(2):
        if p == 1:
            @pl.when(core != 0)
            def _():
                pl.semaphore_wait(turn, 1)

        def to_plane(a, carry, p=p):
            pz = plane(a)
            for py in ys:
                send_pack(p, pz, py)
            return carry

        lax.fori_loop(0, planes - 1, to_plane, 0)
        for py in ys[1:]:
            send_pack(p, z, py)
        pltpu.make_async_copy(
            out_pack.at[p, pl.ds(own_src, unit)],
            in_pack.at[p, pl.ds(own_dst, unit)],
            pack_recv.at[p, me // 16],
        ).start()

    most = (devices - 1) * unit

    def wait_sent(p):
        pltpu.make_async_copy(out_pack.at[p, :most], out_pack.at[p, :most], pack_send.at[p]).wait()

    @pl.when(core == 0)
    def _():
        wait_sent(1)
        pl.semaphore_signal(turn, inc=1, device_id=(me, x * 2 + 1 - core), device_id_type=MESH)

    after = iota((tok, tok), 0) > iota((tok, tok), 1)
    for h in range(heads):
        b_row = buckets_ref[h : h + 1, :]
        b_col = jnp.sum(jnp.where(eye, b_row, 0), axis=1, keepdims=True)
        rank_col = jnp.sum(jnp.where((b_col == b_row) & after, 1, 0), axis=1, keepdims=True)
        pick_buf[h] = one_hot(iota((tok, slots), 1) == b_col * CAP + rank_col)
    loads[3].wait()
    counts = counts_ref[:, y, :]
    spread = (iota((devices, slots), 1) // CAP) == iota((devices, slots), 0)
    rank = lax.rem(iota((1, slots), 1), CAP)
    dead = []
    for j in range(-1, heads):
        b = lax.rem(group * heads + j + devices, devices)
        column = jnp.sum(jnp.where(iota(counts.shape, 1) == b, counts, 0), axis=1, keepdims=True)
        row = jnp.sum(jnp.where(spread, column, 0), axis=0, keepdims=True)
        dead.append(jnp.where(rank < row, 0.0, DEAD))

    def by_bucket(i):
        return i // CAP % 16 * unit + i // part // 2 * (unit // 2) + i // part % 2 * CAP + i % CAP

    order = one_hot(by_bucket(iota((span, span), 0)) == iota((span, span), 1))

    def by_source(i):
        return i // CAP % 16 * unit + i // part * CAP + i % CAP

    order_back = one_hot(by_source(iota((span, span), 1)) == iota((span, span), 0))

    def receive(p):
        for g in range(groups):
            here = in_pack.at[p, g * span : (g + 1) * span]
            pltpu.make_async_copy(here, here, pack_recv.at[p, g]).wait()
            arranged = dot(order, here[...]).astype(BF16)
            for n in range(4):
                j = n % 2 + (heads // 2 if p == 0 else 0)
                rows_buf[j, n // 2, g * part : (g + 1) * part, :] = arranged[n * part : (n + 1) * part]

    receive(0)
    next_z = wrap(z + jnp.where(core == 0, 1, planes - 1), planes)
    to_next = pltpu.make_async_remote_copy(
        src_ref=rows_buf.at[heads - 1],
        dst_ref=prev_buf,
        send_sem=next_send,
        recv_sem=next_recv,
        device_id=(next_z * heads + y, mp),
        device_id_type=MESH,
    )
    to_next.start()

    scale = 1.0 / math.sqrt(dim)
    trans = (((1,), (1,)), ((), ()))

    def attend(j, prev, first, count):
        rows = slice(first, first + count)
        itself = iota((count, slots), 0) + first == iota((count, slots), 1)
        q = rows_buf[j, 0, rows, :]
        own = lax.dot_general(q, rows_buf[j, 0], trans, preferred_element_type=F32) + dead[j + 1]
        own = jnp.where(itself, SELF_SCORE / scale, own)
        far = lax.dot_general(q, prev[0], trans, preferred_element_type=F32) + dead[j]
        top = jnp.maximum(jnp.max(own, axis=1, keepdims=True), jnp.max(far, axis=1, keepdims=True))
        own = jnp.exp2((own - top) * (scale * LOG2E))
        far = jnp.exp2((far - top) * (scale * LOG2E))
        share = 1.0 / (jnp.sum(own, axis=1, keepdims=True) + jnp.sum(far, axis=1, keepdims=True))
        att = dot((own * share).astype(BF16), rows_buf[j, 1]) + dot((far * share).astype(BF16), prev[1])
        att_buf[j, rows, :] = att.astype(BF16)

    attend(heads - 1, rows_buf.at[heads - 2], 0, slots)
    receive(1)

    def send_ret(c, pz, py):
        there = pz * heads + py
        pltpu.make_async_remote_copy(
            src_ref=out_ret.at[pl.ds(pl.multiple_of(there * unit, unit), unit)],
            dst_ref=in_ret.at[pl.ds(own_src, unit)],
            send_sem=ret_send.at[c],
            recv_sem=ret_recv.at[y],
            device_id=(there, mp),
            device_id_type=MESH,
        ).start()

    def send_rest():
        def to_plane(a, carry):
            pz = plane(a)

            @pl.when(pz >= 8)
            def _():
                for py in ys:
                    send_ret(1, pz, py)

            return carry

        lax.fori_loop(0, planes - 1, to_plane, 0)

    for c, (lo, hi) in enumerate(((0, 1), (1, 2), (2, 4))):
        for j in (*range(1, heads - 1), 0):
            if j == 0 and c == 0:
                to_next.wait_recv()
            attend(j, rows_buf.at[j - 1] if j else prev_buf, lo * part, (hi - lo) * part)
        for g in range(lo, hi):
            rows = slice(g * part, (g + 1) * part)
            mine = jnp.concatenate([att_buf[j, rows, :] for j in range(heads)], axis=0)
            out_ret[g * span : (g + 1) * span, :] = dot(order_back, mine).astype(BF16)
        sem = min(c, 1)
        if c < 2:
            for pz in range(4 * lo, 4 * hi):
                @pl.when(z != pz)
                def _(pz=pz):
                    for py in ys:
                        send_ret(sem, pz, py)
        else:
            send_rest()

        @pl.when((z >= 4 * lo) & (z < 4 * hi))
        def _():
            for py in ys[1:]:
                send_ret(sem, z, py)

    pltpu.make_async_copy(
        out_ret.at[pl.ds(own_dst, unit)], in_ret.at[pl.ds(own_src, unit)], ret_recv.at[y]
    ).start()

    loads[4].wait()
    for h in range(heads):
        here = in_ret.at[h * slots : (h + 1) * slots]
        pltpu.make_async_copy(here, here, ret_recv.at[h]).wait()
        tok_buf[:, h * dim : (h + 1) * dim] = dot(pick_buf[h], here[...]).astype(BF16)

    def share_of(m):
        return dot(tok_buf[...], w_buf[:, pl.ds(pl.multiple_of(m * block, block), block)])

    ways = (2, 1, 3, 0)
    quarter = tok // 4

    def give(k):
        cx = lax.rem(x + ways[k], chips)
        pair_out[k] = share_of(cx * 2 + 1 - core).astype(BF16)
        pltpu.make_async_remote_copy(
            src_ref=pair_out.at[k],
            dst_ref=pair_in.at[k],
            send_sem=pair_send,
            recv_sem=pair_recv.at[k],
            device_id=(me, x * 2 + 1 - core),
            device_id_type=MESH,
        ).start()

    def pair_sum(k):
        cx = lax.rem(x + ways[k], chips)
        mine = share_of(cx * 2 + core)
        pltpu.make_async_copy(pair_in.at[k], pair_in.at[k], pair_recv.at[k]).wait()
        return mine + pair_in[k].astype(F32)

    def put(first, rows, way):
        count = rows.shape[0] // quarter
        here = slice(first, first + count)
        chip_out[here] = rows.astype(BF16).reshape(count, quarter, block)
        pltpu.make_async_remote_copy(
            src_ref=chip_out.at[here],
            dst_ref=chip_in.at[here],
            send_sem=chip_send,
            recv_sem=chip_recv.at[first],
            device_id=(me, lax.rem(x + way, chips) * 2 + core),
            device_id_type=MESH,
        ).start()

    def wait_chip(first, count):
        here = chip_in.at[first : first + count]
        pltpu.make_async_copy(here, here, chip_recv.at[first]).wait()

    def part_of(rows, q):
        return rows[q * quarter : (q + 1) * quarter]

    give(0)
    give(1)
    opposite = pair_sum(0)
    for q in (0, 2, 1, 3):
        put(q, part_of(opposite, q), 1 if q < 2 else 3)
    give(2)
    right = pair_sum(1)
    put(4, right[2 * quarter :], 1)
    give(3)
    left = pair_sum(2)
    put(6, left[: 2 * quarter], 3)
    for q in (0, 2, 1, 3):
        wait_chip(q, 1)
        put(8 + q, part_of(right if q < 2 else left, q) + chip_in[q].astype(F32), 1 if q < 2 else 3)
    total = pair_sum(3)
    wait_chip(4, 2)
    wait_chip(6, 2)
    for q in (0, 2, 1, 3):
        near = part_of(total, q) + chip_in[(6, 7, 4, 5)[q]].astype(F32)
        wait_chip(8 + q, 1)
        out_ref[q * quarter : (q + 1) * quarter, :] = (near + chip_in[8 + q].astype(F32)).astype(BF16)

    @pl.when(core != 0)
    def _():
        wait_sent(1)

    wait_sent(0)
    to_next.wait_send()
    @pl.when(z < 4)
    def _():
        here = out_ret.at[: (4 * heads - 1) * unit]
        pltpu.make_async_copy(here, here, ret_send.at[0]).wait()
    @pl.when(z >= 4)
    def _():
        here = out_ret.at[: 4 * heads * unit]
        pltpu.make_async_copy(here, here, ret_send.at[0]).wait()
    @pl.when(z >= 4)
    def _():
        here = out_ret.at[: (12 * heads - 1) * unit]
        pltpu.make_async_copy(here, here, ret_send.at[1]).wait()
    @pl.when(z < 4)
    def _():
        here = out_ret.at[: 12 * heads * unit]
        pltpu.make_async_copy(here, here, ret_send.at[1]).wait()
    pltpu.make_async_copy(pair_out, pair_out, pair_send).wait()
    pltpu.make_async_copy(chip_out, chip_out, chip_send).wait()


def local(planes, chips, shared_qk, values, buckets, counts, w_out):
    buckets = buckets.T
    tok, width = shared_qk.shape
    heads = buckets.shape[0]
    dim = width // heads
    devices = planes * heads
    slots = devices * CAP
    groups = devices // 16
    block = w_out.shape[1] // (2 * chips)
    vmem = pl.BlockSpec(memory_space=pltpu.VMEM)
    dma = pltpu.SemaphoreType.DMA
    return pl.pallas_call(
        functools.partial(layer_kernel, planes, heads, chips, tok, dim),
        out_shape=jax.ShapeDtypeStruct((tok, block), BF16),
        in_specs=[pl.BlockSpec(memory_space=pl.ANY)] * 5,
        out_specs=vmem,
        scratch_shapes=[
            pltpu.VMEM(shared_qk.shape, BF16),
            pltpu.VMEM(values.shape, BF16),
            pltpu.VMEM(buckets.shape, jnp.int32),
            pltpu.VMEM(counts.shape, jnp.int32),
            pltpu.VMEM(w_out.shape, BF16),
            pltpu.VMEM((2, heads * slots, dim), BF16),
            pltpu.VMEM((2, heads * slots, dim), BF16),
            pltpu.VMEM((heads, 2, slots, dim), BF16),
            pltpu.VMEM((2, slots, dim), BF16),
            pltpu.VMEM((heads, slots, dim), BF16),
            pltpu.VMEM((heads * slots, dim), BF16),
            pltpu.VMEM((heads * slots, dim), BF16),
            pltpu.VMEM((tok, heads * dim), BF16),
            pltpu.VMEM((heads, tok, slots), BF16),
            pltpu.VMEM((chips, tok, block), BF16),
            pltpu.VMEM((chips, tok, block), BF16),
            pltpu.VMEM((12, tok // 4, block), BF16),
            pltpu.VMEM((12, tok // 4, block), BF16),
            dma((4,)),
            dma,
            dma((2,)),
            dma((2, groups)),
            dma,
            dma,
            dma((2,)),
            dma((heads,)),
            dma,
            dma((chips,)),
            dma,
            dma((12,)),
            pltpu.SemaphoreType.REGULAR,
        ],
        compiler_params=pltpu.CompilerParams(
            collective_id=0, has_side_effects=True, vmem_limit_bytes=60 * 1024 * 1024
        ),
    )(shared_qk, values, buckets, counts, w_out)


def solution(mesh):
    placed = (P("seq", "mp"), P("seq", "mp"), P("seq", "mp"), P(None, "mp", None), P("mp", None))
    heads = 4
    planes = mesh.shape["seq"] // heads
    chips = mesh.shape["mp"] // 2
    return jax.shard_map(
        functools.partial(local, planes, chips),
        mesh=mesh, in_specs=placed, out_specs=P("seq", "mp"), check_vma=False,
    )
```
